128 devices in a mesh: gx: 4 (over x_hi, core), gy: 32 (over y, z, x_lo).
Axes of the slice: x: 4 (x_hi: 2, x_lo: 2; x = x_hi * 2 + x_lo), y: 4, z: 4, core: 2. Of those that a mesh axis runs over, the one named last changes fastest.
Arguments:
- normed: bfloat16 [512, 14848], P(None, 'gx'), may hold values from -6 to 6
- residual: bfloat16 [512, 14848], P('gy', 'gx'), may hold values from -6 to 6
- w_query: bfloat16 [14848, 4, 32, 64], P('gx', None, 'gy'), may hold values from -0.046875 to 0.046875
- w_keyval: bfloat16 [14848, 4, 256], P('gx', None, 'gy'), may hold values from -0.046875 to 0.046875
- w_out: bfloat16 [32, 4, 64, 14848], P('gy', None, None, 'gx'), may hold values from -0.0625 to 0.0625
- w_up: bfloat16 [14848, 32768], P('gx', 'gy'), may hold values from -0.046875 to 0.046875
- w_down: bfloat16 [32768, 14848], P('gy', 'gx'), may hold values from -0.03125 to 0.03125
- kv_cache: bfloat16 [512, 4, 2, 256, 128], P('gy', 'gx'), may hold values from -300 to 300
- lengths: int32 [512], P('gy'), may hold values from 2 to 256, as said below
Outputs:
- block_out: bfloat16 [512, 14848], P('gy', 'gx')
The draws below stay inside these ranges and needn't reach their ends.
Inputs may be any that keep to these rules, and one draw needn't show every extreme that they name: `lengths`: each sequence has 2 or more cached tokens, and one sequence exactly 256 in every draw.
All inputs are finite; a program needn't handle non-finite values.
Results may differ from the reference program's by a relative error of at most 0.005.
Values may be sent and summed in bfloat16 or wider, within the bound.
A program may use at most 128 MiB of HBM per device.

```python
import jax
import jax.numpy as jnp

D = 14848
FF = 32768
HD = 64
QPG = 16
CTX = 256
QH = 128
SEQS = 512


def draw_kv_cache(key, part):
    key = jax.random.fold_in(key, 11)
    first = jax.random.fold_in(key, 0)
    shape = (SEQS, 4, 2, CTX, 2 * HD)
    return jax.random.normal(first, shape, jnp.float32).astype(jnp.bfloat16)


def draw_lengths(key, part):
    key = jax.random.fold_in(key, 23)
    first, second = jax.random.split(key)
    counts = jax.random.randint(first, (SEQS,), 2, CTX + 1)
    chosen = jax.random.randint(second, (), 0, SEQS)
    return counts.at[chosen].set(CTX).astype(jnp.int32)


def level_of(stream_key, dims, cuts, least, top_value):
    loudness = 1.0
    for dim, shards_of in cuts:
        draws = jax.random.uniform(jax.random.fold_in(jax.random.fold_in(stream_key, 6), dim), (shards_of,), jnp.float32, least / len(cuts), top_value / len(cuts))
        loudness = loudness * jnp.repeat(jnp.exp(draws), dims[dim] // shards_of).reshape((-1,) + (1,) * (len(dims) - 1 - dim))
    return loudness


def gaussian(own_key, shape, deviation, limit, shards=(), dtype=jnp.bfloat16):
    entries = jax.random.normal(own_key, shape, jnp.float32) * deviation
    if len(shards) > 0:
        entries = level_of(own_key, shape, shards, -0.22, 0.18) * entries
    return jnp.clip(entries, min=-limit, max=limit).astype(dtype)


def setup_inputs(seed: int = 0) -> dict:
    splits = jax.random.split(jax.random.key(seed), 10)
    normed = gaussian(splits[0], (SEQS, D), 1.0, 6.0, ((1, 4),))
    residual = gaussian(splits[1], (SEQS, D), 1.0, 6.0, ((0, 32), (1, 4)))
    w_query = gaussian(splits[2], (D, 4, QH // 4, HD), D ** -0.5, 0.046875, ((0, 4), (2, 32)))
    w_keyval = gaussian(splits[3], (D, 4, 4 * HD), D ** -0.5, 0.046875, ((0, 4), (2, 32)))
    w_out = gaussian(splits[4], (QH // 4, 4, HD, D), (QH * HD) ** -0.5, 0.0625, ((0, 32), (3, 4)))
    w_up = gaussian(splits[5], (D, FF), D ** -0.5, 0.046875, ((0, 4), (1, 32)))
    w_down = gaussian(splits[6], (FF, D), FF ** -0.5, 0.03125, ((0, 32), (1, 4)))
    kv_cache = draw_kv_cache(jax.random.fold_in(splits[9], 71), 0)
    lengths = draw_lengths(jax.random.fold_in(splits[9], 71), 0)
    return dict(normed=normed, residual=residual, w_query=w_query, w_keyval=w_keyval, w_out=w_out, w_up=w_up, w_down=w_down, kv_cache=kv_cache, lengths=lengths)


def reference(normed, residual, w_query, w_keyval, w_out, w_up, w_down, kv_cache, lengths):
    query = jnp.dot(normed, w_query.reshape(D, -1), preferred_element_type=jnp.float32)
    query = query.reshape(SEQS, 4, 2, QPG, HD).astype(jnp.bfloat16)
    fresh = jnp.dot(normed, w_keyval.reshape(D, -1), preferred_element_type=jnp.float32)
    fresh = fresh.reshape(SEQS, 4, 2, 2 * HD).astype(jnp.bfloat16)
    up = jnp.dot(normed, w_up, preferred_element_type=jnp.float32)
    hidden = jax.nn.gelu(up, approximate=False).astype(jnp.bfloat16)
    keys = kv_cache[..., :HD].astype(jnp.float32)
    values = kv_cache[..., HD:].astype(jnp.float32)
    qf = query.astype(jnp.float32)
    scores = jnp.einsum("boagd,boald->boagl", qf, keys) * 0.125
    valid = jnp.arange(CTX)[None, None, None, None, :] < lengths[:, None, None, None, None]
    scores = jnp.where(valid, scores, -1e30)
    score_new = jnp.einsum("boagd,boad->boag", qf, fresh[..., :HD].astype(jnp.float32)) * 0.125
    top = jnp.maximum(jnp.max(scores, axis=-1), score_new)
    expo = jnp.exp(scores - top[..., None])
    expo_new = jnp.exp(score_new - top)
    total = jnp.sum(expo, axis=-1) + expo_new
    weight = (expo / total[..., None]).astype(jnp.bfloat16)
    weight_new = (expo_new / total).astype(jnp.bfloat16)
    attended = jnp.einsum("boagl,boald->boagd", weight.astype(jnp.float32), values)
    attended = attended + weight_new.astype(jnp.float32)[..., None] * fresh[:, :, :, None, HD:].astype(jnp.float32)
    attended = attended.astype(jnp.bfloat16).reshape(SEQS, 4, QH // 4, HD)
    flat = jnp.transpose(attended, (0, 2, 1, 3)).reshape(SEQS, QH * HD)
    attn_proj = jnp.dot(flat, w_out.reshape(QH * HD, D), preferred_element_type=jnp.float32)
    ffn_proj = jnp.dot(hidden, w_down, preferred_element_type=jnp.float32)
    return (residual.astype(jnp.float32) + attn_proj + ffn_proj).astype(jnp.bfloat16)
```

```python
import functools

import jax
import jax.numpy as jnp
from jax import lax
from jax.experimental import pallas as pl
from jax.experimental.pallas import tpu as pltpu
from jax.sharding import PartitionSpec as P


MESH = pl.DeviceIdType.MESH


def cdot(a, b):
    return lax.dot_general(a, b, (((1,), (0,)), ((), ())), preferred_element_type=jnp.float32)


def column_chunks(width, lanes):
    tiles = width // 128
    first = (tiles // 2) // 2 * 2
    cols = []
    for lo, hi in ((0, first * 128), (first * 128, width)):
        parts = []
        while lo < hi:
            w = min(lanes, hi - lo)
            parts.append((lo, w))
            lo += w
        cols.append(parts)
    order = []
    for i in range(max(len(cols[0]), len(cols[1]))):
        for s in (0, 1):
            if i < len(cols[s]):
                order.append((s, cols[s][i][0], cols[s][i][1]))
    return order


def down_kernel(chunks, hid_ref, heads_ref, wd_hbm, wo_hbm, out_ref, wd, wo, part, r1, s1, part2, r2, s2, part3, own3, r3,
                wsem, ssem, rsem):
    gx = lax.axis_index("gx")
    gy = lax.axis_index("gy")
    y, z, xl = gy // 8, (gy // 2) % 4, gy % 2

    def at(yy, zz, xx):
        return (gx, (yy * 4 + zz) * 2 + xx)

    ring = (
        (at((y + 1) % 4, z, xl), at((y + 3) % 4, z, xl)),
        (at(y, (z + 1) % 4, xl), at(y, (z + 3) % 4, xl)),
    )
    pair = at(y, z, 1 - xl)
    coord = (y, z)

    loads = []
    for k, (_, c, w) in enumerate(chunks):
        cols = pl.ds(c, w)
        a = pltpu.make_async_copy(wd_hbm.at[:, cols], wd.at[:, cols], wsem.at[2 * k])
        b = pltpu.make_async_copy(wo_hbm.at[:, cols], wo.at[:, cols], wsem.at[2 * k + 1])
        a.start()
        b.start()
        loads.append((a, b))

    barrier = pltpu.get_barrier_semaphore()
    for dev in ring[0] + ring[1] + (pair,):
        pl.semaphore_signal(barrier, inc=1, device_id=dev, device_id_type=MESH)
    pl.semaphore_wait(barrier, 5)

    copies = {}

    def send(k, i, src, dst, dev):
        cp = pltpu.make_async_remote_copy(
            src_ref=src, dst_ref=dst, send_sem=ssem.at[k, i], recv_sem=rsem.at[k, i], device_id=dev, device_id_type=MESH
        )
        cp.start()
        copies[k, i] = cp

    def f32(v):
        return v.astype(jnp.float32)

    def step_compute(k):
        s, c, w = chunks[k]
        cols = pl.ds(c, w)
        p = coord[s]
        plus, minus = ring[s]
        for ld in loads[k]:
            ld.wait()
        acc = cdot(hid_ref[...], wd[:, cols]) + cdot(heads_ref[...], wo[:, cols])
        acc = acc.astype(jnp.bfloat16)
        for i in range(4):
            for j in range(4):
                row = (i * 4 + j) * 32
                if s == 0:
                    part[i, j, :, cols] = acc[row : row + 32]
                else:
                    part[j, i, :, cols] = acc[row : row + 32]
        far, nxt, prv = (p + 2) % 4, (p + 1) % 4, (p + 3) % 4
        send(k, 0, part.at[far, 0:2, :, cols], r1.at[0, :, :, cols], plus)
        send(k, 1, part.at[far, 2:4, :, cols], r1.at[1, :, :, cols], minus)
        send(k, 2, part.at[nxt, 2:4, :, cols], r1.at[2, :, :, cols], plus)
        send(k, 3, part.at[prv, 0:2, :, cols], r1.at[3, :, :, cols], minus)

    def step_relay1(k):
        s, c, w = chunks[k]
        cols = pl.ds(c, w)
        p = coord[s]
        plus, minus = ring[s]
        nxt, prv = (p + 1) % 4, (p + 3) % 4
        copies[k, 0].wait_recv()
        s1[0, :, :, cols] = (f32(r1[0, :, :, cols]) + f32(part[nxt, 0:2, :, cols])).astype(jnp.bfloat16)
        send(k, 4, s1.at[0, :, :, cols], r1.at[4, :, :, cols], plus)
        copies[k, 1].wait_recv()
        s1[1, :, :, cols] = (f32(r1[1, :, :, cols]) + f32(part[prv, 2:4, :, cols])).astype(jnp.bfloat16)
        send(k, 5, s1.at[1, :, :, cols], r1.at[5, :, :, cols], minus)

    def step_second(k):
        s, c, w = chunks[k]
        cols = pl.ds(c, w)
        p, q = coord[s], coord[1 - s]
        plus, minus = ring[1 - s]
        copies[k, 2].wait_recv()
        copies[k, 3].wait_recv()
        copies[k, 4].wait_recv()
        a = f32(part[p, 0:2, :, cols]) + f32(r1[4, :, :, cols]) + f32(r1[3, :, :, cols])
        part2[0:2, :, cols] = a.astype(jnp.bfloat16)
        copies[k, 5].wait_recv()
        b = f32(part[p, 2:4, :, cols]) + f32(r1[5, :, :, cols]) + f32(r1[2, :, :, cols])
        part2[2:4, :, cols] = b.astype(jnp.bfloat16)
        far, nxt, prv = (q + 2) % 4, (q + 1) % 4, (q + 3) % 4
        send(k, 6, part2.at[far, 0:16, cols], r2.at[0, :, cols], plus)
        send(k, 7, part2.at[far, 16:32, cols], r2.at[1, :, cols], minus)
        send(k, 8, part2.at[nxt, 16:32, cols], r2.at[2, :, cols], plus)
        send(k, 9, part2.at[prv, 0:16, cols], r2.at[3, :, cols], minus)

    def step_relay2(k):
        s, c, w = chunks[k]
        cols = pl.ds(c, w)
        q = coord[1 - s]
        plus, minus = ring[1 - s]
        nxt, prv = (q + 1) % 4, (q + 3) % 4
        copies[k, 6].wait_recv()
        s2[0, :, cols] = (f32(r2[0, :, cols]) + f32(part2[nxt, 0:16, cols])).astype(jnp.bfloat16)
        send(k, 10, s2.at[0, :, cols], r2.at[4, :, cols], plus)
        copies[k, 7].wait_recv()
        s2[1, :, cols] = (f32(r2[1, :, cols]) + f32(part2[prv, 16:32, cols])).astype(jnp.bfloat16)
        send(k, 11, s2.at[1, :, cols], r2.at[5, :, cols], minus)

    def step_pair(k):
        s, c, w = chunks[k]
        cols = pl.ds(c, w)
        q = coord[1 - s]
        for i in (8, 9, 10, 11):
            copies[k, i].wait_recv()
        a = f32(part2[q, 0:16, cols]) + f32(r2[4, :, cols]) + f32(r2[3, :, cols])
        b = f32(part2[q, 16:32, cols]) + f32(r2[5, :, cols]) + f32(r2[2, :, cols])
        part3[0, :, cols] = a.astype(jnp.bfloat16)
        part3[1, :, cols] = b.astype(jnp.bfloat16)
        own3[0, :, cols] = a
        own3[1, :, cols] = b
        send(k, 12, part3.at[1 - xl, :, cols], r3.at[:, cols], pair)

    def step_last(k):
        s, c, w = chunks[k]
        cols = pl.ds(c, w)
        copies[k, 12].wait_recv()
        out_ref[:, cols] = own3[xl, :, cols] + f32(r3[:, cols])

    steps = (step_compute, step_relay1, step_second, step_relay2, step_pair, step_last)
    lag = (0, 1, 2, 3, 4, 5)
    n = len(chunks)
    for t in range(n + lag[-1]):
        for fn, d in zip(steps, lag):
            if 0 <= t - d < n:
                fn(t - d)
    for k in range(n):
        for i in range(13):
            copies[k, i].wait_send()


def down_and_scatter(hidden, heads, w_down, w_out, lanes=512):
    width = w_down.shape[1]
    chunks = column_chunks(width, lanes)
    n = len(chunks)
    bf = jnp.bfloat16
    return pl.pallas_call(
        functools.partial(down_kernel, chunks),
        out_shape=jax.ShapeDtypeStruct((16, width), jnp.float32),
        in_specs=[
            pl.BlockSpec(memory_space=pltpu.VMEM),
            pl.BlockSpec(memory_space=pltpu.VMEM),
            pl.BlockSpec(memory_space=pl.ANY),
            pl.BlockSpec(memory_space=pl.ANY),
        ],
        out_specs=pl.BlockSpec(memory_space=pltpu.VMEM),
        scratch_shapes=[
            pltpu.VMEM(w_down.shape, bf),
            pltpu.VMEM(w_out.shape, bf),
            pltpu.VMEM((4, 4, 32, width), bf),
            pltpu.VMEM((6, 2, 32, width), bf),
            pltpu.VMEM((2, 2, 32, width), bf),
            pltpu.VMEM((4, 32, width), bf),
            pltpu.VMEM((6, 16, width), bf),
            pltpu.VMEM((2, 16, width), bf),
            pltpu.VMEM((2, 16, width), bf),
            pltpu.VMEM((2, 16, width), jnp.float32),
            pltpu.VMEM((16, width), bf),
            pltpu.SemaphoreType.DMA((2 * n,)),
            pltpu.SemaphoreType.DMA((n, 13)),
            pltpu.SemaphoreType.DMA((n, 13)),
        ],
        compiler_params=pltpu.CompilerParams(
            collective_id=1, has_side_effects=True, vmem_limit_bytes=56 * 1024 * 1024
        ),
        cost_estimate=pl.CostEstimate(
            flops=2 * 512 * 1280 * width, bytes_accessed=2 * 1280 * width, transcendentals=0
        ),
    )(hidden, heads, w_down, w_out)


def attend(q_mine, kv_mine, cache, lengths):
    seqs = q_mine.shape[0]
    heads = q_mine.shape[2]
    head_dim = q_mine.shape[3]
    span = cache.shape[3]
    query = q_mine.reshape(seqs, 2, heads // 2, head_dim)
    fresh = kv_mine.reshape(seqs, 2, 2 * head_dim)
    local = cache[:, 0]
    keys = local[..., :head_dim]
    values = local[..., head_dim:]
    scores = jnp.einsum("bagd,bald->bagl", query, keys, preferred_element_type=jnp.float32) * 0.125
    valid = jnp.arange(span)[None, None, None, :] < lengths[:, None, None, None]
    scores = jnp.where(valid, scores, -1e30)
    score_new = (
        jnp.einsum(
            "bagd,bad->bag", query, fresh[..., :head_dim], preferred_element_type=jnp.float32
        )
        * 0.125
    )
    top = jnp.maximum(jnp.max(scores, axis=-1), score_new)
    expo = jnp.exp(scores - top[..., None])
    expo_new = jnp.exp(score_new - top)
    total = jnp.sum(expo, axis=-1) + expo_new
    weight = (expo / total[..., None]).astype(jnp.bfloat16)
    weight_new = (expo_new / total).astype(jnp.bfloat16)
    attended = jnp.einsum("bagl,bald->bagd", weight, values, preferred_element_type=jnp.float32)
    attended = attended + weight_new.astype(jnp.float32)[..., None] * fresh[
        :, :, None, head_dim:
    ].astype(jnp.float32)
    return attended.astype(jnp.bfloat16).reshape(seqs, 1, heads, head_dim)


def on_device(normed, residual, w_query, w_keyval, w_out, w_up, w_down, kv_cache, lengths):
    rows = normed.shape[0]
    width = normed.shape[1]
    slots = w_query.shape[2]
    head_dim = w_query.shape[3]
    kv_cols = w_keyval.shape[2]
    q_part = jnp.dot(normed, w_query.reshape(width, -1), preferred_element_type=jnp.float32)
    q_part = q_part.reshape(rows, 4, slots, head_dim)
    kv_part = jnp.dot(normed, w_keyval.reshape(width, -1), preferred_element_type=jnp.float32)
    kv_part = kv_part.reshape(rows, 4, kv_cols)
    up_part = jnp.dot(normed, w_up, preferred_element_type=jnp.float32)
    q_all, kv_all, up_all = lax.psum((q_part, kv_part, up_part), "gx")
    q_send = q_all.astype(jnp.bfloat16)
    kv_send = kv_all.astype(jnp.bfloat16).reshape(rows, 4, kv_cols, 1)
    hidden = jax.nn.gelu(up_all, approximate=False).astype(jnp.bfloat16)
    q_pairs, kv_pairs = (
        lax.all_to_all(q_send, "gy", split_axis=0, concat_axis=2, tiled=True),
        lax.all_to_all(kv_send, "gy", split_axis=0, concat_axis=2, tiled=True),
    )
    owner = lax.axis_index("gx")
    q_mine = lax.dynamic_slice_in_dim(q_pairs, owner, 1, 1)
    kv_mine = lax.dynamic_slice_in_dim(kv_pairs, owner, 1, 1)
    attended = attend(q_mine, kv_mine, kv_cache, lengths)
    returned = lax.all_to_all(attended, "gy", split_axis=2, concat_axis=0, tiled=True)
    heads_all = lax.all_gather(returned, "gx", axis=1, tiled=True)
    summed = down_and_scatter(
        hidden, heads_all.reshape(rows, -1), w_down, w_out.reshape(-1, w_out.shape[3])
    )
    return (residual.astype(jnp.float32) + summed).astype(jnp.bfloat16)


def solution(mesh):
    placed = (
        P(None, "gx"),
        P("gy", "gx"),
        P("gx", None, "gy", None),
        P("gx", None, "gy"),
        P("gy", None, None, "gx"),
        P("gx", "gy"),
        P("gy", "gx"),
        P("gy", "gx", None, None, None),
        P("gy"),
    )
    return jax.shard_map(
        on_device, mesh=mesh, in_specs=placed, out_specs=P("gy", "gx"), check_vma=False
    )
```

```python
import functools

import jax
import jax.numpy as jnp
from jax import lax
from jax.experimental import pallas as pl
from jax.experimental.pallas import tpu as pltpu
from jax.sharding import PartitionSpec as P

MESH = pl.DeviceIdType.MESH


def cdot(a, b):
    return lax.dot_general(a, b, (((1,), (0,)), ((), ())), preferred_element_type=jnp.float32)


def column_chunks(width, lanes):
    tiles = width // 128
    first = (tiles // 2) // 2 * 2
    cols = []
    for lo, hi in ((0, first * 128), (first * 128, width)):
        parts = []
        while lo < hi:
            w = min(lanes, hi - lo)
            parts.append((lo, w))
            lo += w
        cols.append(parts)
    order = []
    for i in range(max(len(cols[0]), len(cols[1]))):
        for s in (0, 1):
            if i < len(cols[s]):
                order.append((s, cols[s][i][0], cols[s][i][1]))
    return order


def down_kernel(chunks, hid_ref, heads_ref, wd_hbm, wo_hbm, out_ref, wd, wo, part, r1, s1, part2, r2, s2, part3, own3, r3,
                wsem, ssem, rsem):
    gx = lax.axis_index("gx")
    gy = lax.axis_index("gy")
    y, z, xl = gy // 8, (gy // 2) % 4, gy % 2

    def at(yy, zz, xx):
        return (gx, (yy * 4 + zz) * 2 + xx)

    ring = (
        (at((y + 1) % 4, z, xl), at((y + 3) % 4, z, xl)),
        (at(y, (z + 1) % 4, xl), at(y, (z + 3) % 4, xl)),
    )
    pair = at(y, z, 1 - xl)
    coord = (y, z)

    loads = []
    for k, (_, c, w) in enumerate(chunks):
        cols = pl.ds(c, w)
        a = pltpu.make_async_copy(wd_hbm.at[:, cols], wd.at[:, cols], wsem.at[2 * k])
        b = pltpu.make_async_copy(wo_hbm.at[:, cols], wo.at[:, cols], wsem.at[2 * k + 1])
        a.start()
        b.start()
        loads.append((a, b))

    barrier = pltpu.get_barrier_semaphore()
    for dev in ring[0] + ring[1] + (pair,):
        pl.semaphore_signal(barrier, inc=1, device_id=dev, device_id_type=MESH)
    pl.semaphore_wait(barrier, 5)

    copies = {}

    def send(k, i, src, dst, dev):
        cp = pltpu.make_async_remote_copy(
            src_ref=src, dst_ref=dst, send_sem=ssem.at[k, i], recv_sem=rsem.at[k, i], device_id=dev, device_id_type=MESH
        )
        cp.start()
        copies[k, i] = cp

    def f32(v):
        return v.astype(jnp.float32)

    def step_compute(k):
        s, c, w = chunks[k]
        cols = pl.ds(c, w)
        p = coord[s]
        plus, minus = ring[s]
        for ld in loads[k]:
            ld.wait()
        acc = cdot(hid_ref[...], wd[:, cols]) + cdot(heads_ref[...], wo[:, cols])
        acc = acc.astype(jnp.bfloat16)
        for i in range(4):
            for j in range(4):
                row = (i * 4 + j) * 32
                if s == 0:
                    part[i, j, :, cols] = acc[row : row + 32]
                else:
                    part[j, i, :, cols] = acc[row : row + 32]
        far, nxt, prv = (p + 2) % 4, (p + 1) % 4, (p + 3) % 4
        send(k, 0, part.at[far, 0:2, :, cols], r1.at[0, :, :, cols], plus)
        send(k, 1, part.at[far, 2:4, :, cols], r1.at[1, :, :, cols], minus)
        send(k, 2, part.at[nxt, 2:4, :, cols], r1.at[2, :, :, cols], plus)
        send(k, 3, part.at[prv, 0:2, :, cols], r1.at[3, :, :, cols], minus)

    def step_relay1(k):
        s, c, w = chunks[k]
        cols = pl.ds(c, w)
        p = coord[s]
        plus, minus = ring[s]
        nxt, prv = (p + 1) % 4, (p + 3) % 4
        copies[k, 0].wait_recv()
        s1[0, :, :, cols] = (f32(r1[0, :, :, cols]) + f32(part[nxt, 0:2, :, cols])).astype(jnp.bfloat16)
        send(k, 4, s1.at[0, :, :, cols], r1.at[4, :, :, cols], plus)
        copies[k, 1].wait_recv()
        s1[1, :, :, cols] = (f32(r1[1, :, :, cols]) + f32(part[prv, 2:4, :, cols])).astype(jnp.bfloat16)
        send(k, 5, s1.at[1, :, :, cols], r1.at[5, :, :, cols], minus)

    def step_second(k):
        s, c, w = chunks[k]
        cols = pl.ds(c, w)
        p, q = coord[s], coord[1 - s]
        plus, minus = ring[1 - s]
        copies[k, 2].wait_recv()
        copies[k, 3].wait_recv()
        copies[k, 4].wait_recv()
        a = f32(part[p, 0:2, :, cols]) + f32(r1[4, :, :, cols]) + f32(r1[3, :, :, cols])
        part2[0:2, :, cols] = a.astype(jnp.bfloat16)
        copies[k, 5].wait_recv()
        b = f32(part[p, 2:4, :, cols]) + f32(r1[5, :, :, cols]) + f32(r1[2, :, :, cols])
        part2[2:4, :, cols] = b.astype(jnp.bfloat16)
        far, nxt, prv = (q + 2) % 4, (q + 1) % 4, (q + 3) % 4
        send(k, 6, part2.at[far, 0:16, cols], r2.at[0, :, cols], plus)
        send(k, 7, part2.at[far, 16:32, cols], r2.at[1, :, cols], minus)
        send(k, 8, part2.at[nxt, 16:32, cols], r2.at[2, :, cols], plus)
        send(k, 9, part2.at[prv, 0:16, cols], r2.at[3, :, cols], minus)

    def step_relay2(k):
        s, c, w = chunks[k]
        cols = pl.ds(c, w)
        q = coord[1 - s]
        plus, minus = ring[1 - s]
        nxt, prv = (q + 1) % 4, (q + 3) % 4
        copies[k, 6].wait_recv()
        s2[0, :, cols] = (f32(r2[0, :, cols]) + f32(part2[nxt, 0:16, cols])).astype(jnp.bfloat16)
        send(k, 10, s2.at[0, :, cols], r2.at[4, :, cols], plus)
        copies[k, 7].wait_recv()
        s2[1, :, cols] = (f32(r2[1, :, cols]) + f32(part2[prv, 16:32, cols])).astype(jnp.bfloat16)
        send(k, 11, s2.at[1, :, cols], r2.at[5, :, cols], minus)

    def step_pair(k):
        s, c, w = chunks[k]
        cols = pl.ds(c, w)
        q = coord[1 - s]
        for i in (8, 9, 10, 11):
            copies[k, i].wait_recv()
        a = f32(part2[q, 0:16, cols]) + f32(r2[4, :, cols]) + f32(r2[3, :, cols])
        b = f32(part2[q, 16:32, cols]) + f32(r2[5, :, cols]) + f32(r2[2, :, cols])
        part3[0, :, cols] = a.astype(jnp.bfloat16)
        part3[1, :, cols] = b.astype(jnp.bfloat16)
        own3[0, :, cols] = a
        own3[1, :, cols] = b
        send(k, 12, part3.at[1 - xl, :, cols], r3.at[:, cols], pair)

    def step_last(k):
        s, c, w = chunks[k]
        cols = pl.ds(c, w)
        copies[k, 12].wait_recv()
        out_ref[:, cols] = own3[xl, :, cols] + f32(r3[:, cols])

    steps = (step_compute, step_relay1, step_second, step_relay2, step_pair, step_last)
    lag = (0, 1, 2, 3, 4, 5)
    n = len(chunks)
    for t in range(n + lag[-1]):
        for fn, d in zip(steps, lag):
            if 0 <= t - d < n:
                fn(t - d)
    for k in range(n):
        for i in range(13):
            copies[k, i].wait_send()


def down_and_scatter(hidden, heads, w_down, w_out, lanes=512):
    width = w_down.shape[1]
    chunks = column_chunks(width, lanes)
    n = len(chunks)
    bf = jnp.bfloat16
    return pl.pallas_call(
        functools.partial(down_kernel, chunks),
        out_shape=jax.ShapeDtypeStruct((16, width), jnp.float32),
        in_specs=[
            pl.BlockSpec(memory_space=pltpu.VMEM),
            pl.BlockSpec(memory_space=pltpu.VMEM),
            pl.BlockSpec(memory_space=pl.ANY),
            pl.BlockSpec(memory_space=pl.ANY),
        ],
        out_specs=pl.BlockSpec(memory_space=pltpu.VMEM),
        scratch_shapes=[
            pltpu.VMEM(w_down.shape, bf),
            pltpu.VMEM(w_out.shape, bf),
            pltpu.VMEM((4, 4, 32, width), bf),
            pltpu.VMEM((6, 2, 32, width), bf),
            pltpu.VMEM((2, 2, 32, width), bf),
            pltpu.VMEM((4, 32, width), bf),
            pltpu.VMEM((6, 16, width), bf),
            pltpu.VMEM((2, 16, width), bf),
            pltpu.VMEM((2, 16, width), bf),
            pltpu.VMEM((2, 16, width), jnp.float32),
            pltpu.VMEM((16, width), bf),
            pltpu.SemaphoreType.DMA((2 * n,)),
            pltpu.SemaphoreType.DMA((n, 13)),
            pltpu.SemaphoreType.DMA((n, 13)),
        ],
        compiler_params=pltpu.CompilerParams(
            collective_id=1, has_side_effects=True, vmem_limit_bytes=56 * 1024 * 1024
        ),
        cost_estimate=pl.CostEstimate(
            flops=2 * 512 * 1280 * width, bytes_accessed=2 * 1280 * width, transcendentals=0
        ),
    )(hidden, heads, w_down, w_out)


def tdot(a, b):
    return lax.dot_general(a, b, (((1,), (1,)), ((), ())), preferred_element_type=jnp.float32)


def iotas(shape):
    return lax.broadcasted_iota(jnp.int32, shape, 0), lax.broadcasted_iota(jnp.int32, shape, 1)


def one_hot(mask):
    return jnp.where(mask, 1.0, 0.0).astype(jnp.bfloat16)


def front_kernel(len_ref, x_hbm, wq_hbm, wkv_hbm, wu_hbm, kv_hbm, hid_out, heads_out, xv, wq, wkv, wu, kv, qpart, qr1, qs, qr2,
                 qa, qrecv, us, ur, xs, ux, own, hid, perm, iperm, ss, wv, att, asend, hrecv, heads4, wsem, ssem, rsem, asem, brecv):
    bf = jnp.bfloat16
    gx = lax.axis_index("gx")
    gy = lax.axis_index("gy")
    xh, c = gx // 2, gx % 2
    core = (xh * 2 + 1 - c, gy)
    far = ((1 - xh) * 2 + c, gy)
    order = ((1 - xh) * 2 + 1 - c, (1 - xh) * 2 + c, xh * 2 + 1 - c, gx)

    def quarter(g):
        return pl.ds(pl.multiple_of(g * 256, 256), 256)

    loads = [
        pltpu.make_async_copy(x_hbm, xv, wsem.at[0]),
        pltpu.make_async_copy(wq_hbm, wq, wsem.at[1]),
        pltpu.make_async_copy(wkv_hbm, wkv, wsem.at[2]),
    ]
    for i in range(4):
        loads.append(pltpu.make_async_copy(wu_hbm.at[:, quarter(order[i])], wu.at[i], wsem.at[3 + i]))
    loads.append(pltpu.make_async_copy(kv_hbm, kv, wsem.at[7]))
    for ld in loads:
        ld.start()

    barrier = pltpu.get_barrier_semaphore()
    pl.semaphore_signal(barrier, inc=1, device_id=core, device_id_type=MESH)
    pl.semaphore_signal(barrier, inc=1, device_id=far, device_id_type=MESH)

    def greet(i, carry):
        pl.semaphore_signal(barrier, inc=1, device_id=(gx, (gy + i) % 32), device_id_type=MESH)
        return carry

    lax.fori_loop(1, 32, greet, 0)

    r, k = iotas((512, 512))
    perm[...] = one_hot(k == (r % 32) * 16 + r // 32)
    iperm[...] = one_hot(k == (r % 16) * 32 + r // 16)

    pl.semaphore_wait(barrier, 33)

    copies = {}

    def send(i, src, dst, dev):
        cp = pltpu.make_async_remote_copy(
            src_ref=src, dst_ref=dst, send_sem=ssem.at[i], recv_sem=rsem.at[i], device_id=dev, device_id_type=MESH
        )
        cp.start()
        copies[i] = cp

    for ld in loads[:3]:
        ld.wait()
    qt = tdot(wq[...], xv[...])
    kvt = tdot(wkv[...], xv[...])
    for o in range(4):
        qpart[o // 2, o % 2, 0:64, :] = qt[o * 64 : o * 64 + 64]
        qpart[o // 2, o % 2, 64:72, :] = kvt[o * 8 : o * 8 + 8]
    send(0, qpart.at[1 - xh, 1 - c], qr1.at[0], core)
    send(1, qpart.at[xh, 1 - c], qr1.at[1], core)

    loads[3].wait()
    us[0] = cdot(xv[...], wu[0]).astype(bf)
    send(2, us.at[0], ur.at[0], core)

    copies[0].wait_recv()
    qs[...] = qpart[1 - xh, c] + qr1[0]
    send(3, qs, qr2, far)

    loads[4].wait()
    up = cdot(xv[...], wu[1])
    copies[2].wait_recv()
    xs[...] = (up + ur[0].astype(jnp.float32)).astype(bf)
    send(4, xs.at[0:256], ux.at[0:256], far)
    send(5, xs.at[256:512], ux.at[256:512], far)

    loads[5].wait()
    us[1] = cdot(xv[...], wu[2]).astype(bf)
    send(6, us.at[1], ur.at[1], core)

    copies[1].wait_recv()
    copies[3].wait_recv()
    qsum = qpart[xh, c] + qr1[1] + qr2[...]
    qrows = jnp.concatenate([qsum, jnp.zeros((56, 512), jnp.float32)], axis=0).T
    qa[...] = qrows.astype(bf).reshape(32, 16, 128)
    qrecv[gy] = qa[gy]

    def hop(which, src, dst):
        def body(i, carry):
            peer = (gy + i) % 32
            pltpu.make_async_remote_copy(
                src_ref=src.at[peer],
                dst_ref=dst.at[gy],
                send_sem=asem.at[which, i],
                recv_sem=brecv.at[which, i],
                device_id=(gx, peer),
                device_id_type=MESH,
            ).start()
            return carry

        lax.fori_loop(1, 32, body, 0)

    def hop_copy(which, src, dst, i):
        peer = (gy + i) % 32
        return pltpu.make_async_remote_copy(
            src_ref=src.at[peer],
            dst_ref=dst.at[(gy + 32 - i) % 32],
            send_sem=asem.at[which, i],
            recv_sem=brecv.at[which, i],
            device_id=(gx, peer),
            device_id_type=MESH,
        )

    def hop_recv(which, src, dst):
        def body(i, carry):
            hop_copy(which, src, dst, i).wait_recv()
            return carry

        lax.fori_loop(1, 32, body, 0)

    def hop_sent(which, src, dst):
        def body(i, carry):
            hop_copy(which, src, dst, i).wait_send()
            return carry

        lax.fori_loop(1, 32, body, 0)

    hop(0, qa, qrecv)

    loads[6].wait()
    own[...] = cdot(xv[...], wu[3])
    copies[6].wait_recv()
    own[...] += ur[1].astype(jnp.float32)
    loads[7].wait()

    hop_recv(0, qa, qrecv)
    qall = qrecv[...].reshape(512, 128)
    k2, j2 = iotas((128, 256))
    spread = cdot(qall, one_hot(k2 - 64 == j2 % 8))
    r3, j3 = iotas((512, 256))
    spread = jnp.where(j3 // 8 == r3 // 16, spread, 0.0).astype(bf)
    b4, r4 = iotas((16, 512))
    fresh = cdot(one_hot(r4 % 16 == b4), spread).astype(bf)
    fr = jnp.concatenate([fresh[:, 0:128], fresh[:, 128:256]], axis=0)
    qp = cdot(perm[...], qall)
    _, lane = iotas((512, 128))
    q128 = jnp.where(lane < 64, qp, 0.0).astype(bf)
    _, pos = iotas((16, 256))
    for b in range(16):
        ln = len_ref[b]
        for a in range(2):
            row = b * 32 + a * 16
            sc = tdot(q128[row : row + 16], kv[b, a]) * 0.125
            ss[row : row + 16, :] = jnp.where(pos < ln, sc, -1e30)
    sn = tdot(q128, fr) * 0.125
    r5, j5 = iotas((512, 32))
    match = j5 == ((r5 // 16) % 2) * 16 + r5 // 32
    sn = jnp.sum(jnp.where(match, sn, 0.0), axis=1, keepdims=True)
    wns = []
    for i in range(4):
        blk = ss[i * 128 : (i + 1) * 128, :]
        new = sn[i * 128 : (i + 1) * 128]
        top = jnp.maximum(jnp.max(blk, axis=1, keepdims=True), new)
        e = jnp.exp(blk - top)
        en = jnp.exp(new - top)
        tot = jnp.sum(e, axis=1, keepdims=True) + en
        wv[i * 128 : (i + 1) * 128, :] = (e / tot).astype(bf)
        wns.append(en / tot)
    wn = jnp.concatenate(wns, axis=0)
    wnm = jnp.where(match, wn, 0.0).astype(bf)
    for b in range(16):
        for a in range(2):
            row = b * 32 + a * 16
            att[row : row + 16, :] = cdot(wv[row : row + 16, :], kv[b, a])
    atted = (att[...] + cdot(wnm, fr)).astype(bf)
    asend[...] = cdot(iperm[...], atted).astype(bf).reshape(32, 16, 128)
    hrecv[gy] = asend[gy]
    hop(1, asend, hrecv)

    for h in range(2):
        rows = slice(h * 256, h * 256 + 256)
        copies[4 + h].wait_recv()
        v = own[rows, :] + ux[rows, :].astype(jnp.float32)
        v = 0.5 * v * (1.0 + lax.erf(v * 0.7071067811865476))
        hid[rows, quarter(gx)] = v.astype(bf)
        send(7 + h, hid.at[rows, quarter(gx)], hid.at[rows, quarter(gx)], far)
        send(9 + h, hid.at[rows, quarter(gx)], hid.at[rows, quarter(gx)], core)

    hop_recv(1, asend, hrecv)
    heads4[gx] = hrecv[...].reshape(512, 128)
    send(11, heads4.at[gx], heads4.at[gx], far)
    send(12, heads4.at[gx], heads4.at[gx], core)

    g = (1 - xh) * 2 + c
    for h in range(2):
        rows = slice(h * 256, h * 256 + 256)
        copies[7 + h].wait_recv()
        send(13 + h, hid.at[rows, quarter(g)], hid.at[rows, quarter(g)], core)
    copies[11].wait_recv()
    send(15, heads4.at[g], heads4.at[g], core)
    copies[12].wait_recv()
    for i in (9, 10, 13, 14, 15):
        copies[i].wait_recv()
    heads_out[...] = jnp.concatenate([heads4[o][:, 64:128] for o in range(4)], axis=1)
    hid_out[...] = hid[...]
    for i in range(16):
        copies[i].wait_send()
    hop_sent(0, qa, qrecv)
    hop_sent(1, asend, hrecv)


def front(normed, w_query, w_keyval, w_up, kv_cache, lengths):
    width = normed.shape[1]
    bf, f4 = jnp.bfloat16, jnp.float32
    V = pltpu.VMEM
    wq = jnp.transpose(w_query, (1, 2, 3, 0)).reshape(-1, width)
    wkv = jnp.transpose(w_keyval, (1, 2, 0)).reshape(-1, width)
    kv = kv_cache.reshape(16, 2, 256, 128)
    hbm = pl.BlockSpec(memory_space=pl.ANY)
    vm = pl.BlockSpec(memory_space=pltpu.VMEM)
    return pl.pallas_call(
        front_kernel,
        out_shape=(jax.ShapeDtypeStruct((512, 1024), bf), jax.ShapeDtypeStruct((512, 256), bf)),
        in_specs=[pl.BlockSpec(memory_space=pltpu.SMEM)] + [hbm] * 5,
        out_specs=(vm, vm),
        scratch_shapes=[
            V((512, width), bf),
            V((256, width), bf),
            V((32, width), bf),
            V((4, width, 256), bf),
            V((16, 2, 256, 128), bf),
            V((2, 2, 72, 512), f4),
            V((2, 72, 512), f4),
            V((72, 512), f4),
            V((72, 512), f4),
            V((32, 16, 128), bf),
            V((32, 16, 128), bf),
            V((2, 512, 256), bf),
            V((2, 512, 256), bf),
            V((512, 256), bf),
            V((512, 256), bf),
            V((512, 256), f4),
            V((512, 1024), bf),
            V((512, 512), bf),
            V((512, 512), bf),
            V((512, 256), f4),
            V((512, 256), bf),
            V((512, 128), f4),
            V((32, 16, 128), bf),
            V((32, 16, 128), bf),
            V((4, 512, 128), bf),
            pltpu.SemaphoreType.DMA((8,)),
            pltpu.SemaphoreType.DMA((16,)),
            pltpu.SemaphoreType.DMA((16,)),
            pltpu.SemaphoreType.DMA((2, 32)),
            pltpu.SemaphoreType.DMA((2, 32)),
        ],
        compiler_params=pltpu.CompilerParams(
            collective_id=2, has_side_effects=True, vmem_limit_bytes=56 * 1024 * 1024
        ),
        cost_estimate=pl.CostEstimate(
            flops=2 * 512 * 1312 * width, bytes_accessed=2 * 1824 * width, transcendentals=0
        ),
    )(lengths, normed, wq, wkv, w_up, kv)


def on_device(normed, residual, w_query, w_keyval, w_out, w_up, w_down, kv_cache, lengths):
    hidden, heads = front(normed, w_query, w_keyval, w_up, kv_cache, lengths)
    summed = down_and_scatter(hidden, heads, w_down, w_out.reshape(-1, w_out.shape[3]))
    return (residual.astype(jnp.float32) + summed).astype(jnp.bfloat16)


def solution(mesh):
    placed = (
        P(None, "gx"),
        P("gy", "gx"),
        P("gx", None, "gy", None),
        P("gx", None, "gy"),
        P("gy", None, None, "gx"),
        P("gx", "gy"),
        P("gy", "gx"),
        P("gy", "gx", None, None, None),
        P("gy"),
    )
    return jax.shard_map(
        on_device, mesh=mesh, in_specs=placed, out_specs=P("gy", "gx"), check_vma=False
    )
```

```python
import functools

import jax
import jax.numpy as jnp
from jax import lax
from jax.experimental import pallas as pl
from jax.experimental.pallas import tpu as pltpu
from jax.sharding import PartitionSpec as P

MESH = pl.DeviceIdType.MESH


def cdot(a, b):
    return lax.dot_general(a, b, (((1,), (0,)), ((), ())), preferred_element_type=jnp.float32)


def column_chunks(width, lanes):
    tiles = width // 128
    first = (tiles // 2) // 2 * 2
    cols = []
    for lo, hi in ((0, first * 128), (first * 128, width)):
        parts = []
        while lo < hi:
            w = min(lanes, hi - lo)
            parts.append((lo, w))
            lo += w
        cols.append(parts)
    order = []
    for i in range(max(len(cols[0]), len(cols[1]))):
        for s in (0, 1):
            if i < len(cols[s]):
                order.append((s, cols[s][i][0], cols[s][i][1]))
    return order


def tdot(a, b):
    return lax.dot_general(a, b, (((1,), (1,)), ((), ())), preferred_element_type=jnp.float32)


def iotas(shape):
    return lax.broadcasted_iota(jnp.int32, shape, 0), lax.broadcasted_iota(jnp.int32, shape, 1)


def one_hot(mask):
    return jnp.where(mask, 1.0, 0.0).astype(jnp.bfloat16)


def layer_kernel(chunks, lag, len_ref, x_hbm, wq_hbm, wkv_hbm, wu_hbm, kv_hbm, wd_hbm, wo_hbm, out_ref,
                 xv, wq, wkv, wu, kv, qpart, qr1, qs, qr2, qa, qrecv, us, ur, xs, ux, own, act, perm, iperm, ss, wv, att, asend,
                 hrecv, heads4, wd, part, r1, s1, part2, r2, s2, part3, own3, r3, wsem, fsend, frecv, asem, brecv, ssem, rsem):
    bf = jnp.bfloat16
    gx = lax.axis_index("gx")
    gy = lax.axis_index("gy")
    xh, c = gx // 2, gx % 2
    y, z, xl = gy // 8, (gy // 2) % 4, gy % 2
    core = (xh * 2 + 1 - c, gy)
    far = ((1 - xh) * 2 + c, gy)
    order = ((1 - xh) * 2 + 1 - c, (1 - xh) * 2 + c, xh * 2 + 1 - c, gx)

    def f32(v):
        return v.astype(jnp.float32)

    def quarter(g):
        return pl.ds(pl.multiple_of(g * 256, 256), 256)

    loads = [
        pltpu.make_async_copy(x_hbm, xv, wsem.at[0]),
        pltpu.make_async_copy(wq_hbm, wq, wsem.at[1]),
        pltpu.make_async_copy(wkv_hbm, wkv, wsem.at[2]),
    ]
    for i in range(4):
        loads.append(pltpu.make_async_copy(wu_hbm.at[:, quarter(order[i])], wu.at[i], wsem.at[3 + i]))
    loads.append(pltpu.make_async_copy(kv_hbm, kv, wsem.at[7]))
    for ld in loads:
        ld.start()
    late = []
    for k, (_, lo, w) in enumerate(chunks):
        cols = pl.ds(lo, w)
        late.append(
            (
                pltpu.make_async_copy(wd_hbm.at[:, cols], wd.at[0:1024, cols], wsem.at[8 + 2 * k]),
                pltpu.make_async_copy(wo_hbm.at[:, cols], wd.at[1024:1280, cols], wsem.at[9 + 2 * k]),
            )
        )

    barrier = pltpu.get_barrier_semaphore()
    pl.semaphore_signal(barrier, inc=1, device_id=core, device_id_type=MESH)
    pl.semaphore_signal(barrier, inc=1, device_id=far, device_id_type=MESH)

    def greet(i, carry):
        pl.semaphore_signal(barrier, inc=1, device_id=(gx, (gy + i) % 32), device_id_type=MESH)
        return carry

    lax.fori_loop(1, 32, greet, 0)

    moved = {}

    def move(i, src, dst, dev):
        cp = pltpu.make_async_remote_copy(
            src_ref=src, dst_ref=dst, send_sem=fsend.at[i], recv_sem=frecv.at[i], device_id=dev, device_id_type=MESH
        )
        cp.start()
        moved[i] = cp

    for ld in loads[:3]:
        ld.wait()
    qt = tdot(wq[...], xv[...])
    kvt = tdot(wkv[...], xv[...])
    for o in range(4):
        qpart[o // 2, o % 2, 0:64, :] = qt[o * 64 : o * 64 + 64]
        qpart[o // 2, o % 2, 64:72, :] = kvt[o * 8 : o * 8 + 8]
    pl.semaphore_wait(barrier, 33)
    move(0, qpart.at[1 - xh, 1 - c], qr1.at[0], core)
    move(1, qpart.at[xh, 1 - c], qr1.at[1], core)

    loads[3].wait()
    us[0] = cdot(xv[...], wu[0]).astype(bf)
    move(2, us.at[0], ur.at[0], core)

    moved[0].wait_recv()
    qs[...] = qpart[1 - xh, c] + qr1[0]
    move(3, qs, qr2, far)

    loads[4].wait()
    up = cdot(xv[...], wu[1])
    moved[2].wait_recv()
    xs[...] = (up + f32(ur[0])).astype(bf)
    for h in range(4):
        rows = slice(h * 128, h * 128 + 128)
        move(4 + h, xs.at[rows], ux.at[rows], far)

    for a, b in late:
        a.start()
        b.start()

    loads[5].wait()
    us[1] = cdot(xv[...], wu[2]).astype(bf)
    move(8, us.at[1], ur.at[1], core)

    r, k = iotas((512, 512))
    perm[...] = one_hot(k == (r % 32) * 16 + r // 32)
    iperm[...] = one_hot(k == (r % 16) * 32 + r // 16)

    moved[1].wait_recv()
    moved[3].wait_recv()
    qsum = qpart[xh, c] + qr1[1] + qr2[...]
    qrows = jnp.concatenate([qsum, jnp.zeros((56, 512), jnp.float32)], axis=0).T
    qa[...] = qrows.astype(bf).reshape(32, 16, 128)
    qrecv[gy] = qa[gy]

    def hop_copy(which, src, dst, i, slot):
        peer = (gy + i) % 32
        return pltpu.make_async_remote_copy(
            src_ref=src.at[peer],
            dst_ref=dst.at[slot],
            send_sem=asem.at[which, i],
            recv_sem=brecv.at[which, i],
            device_id=(gx, peer),
            device_id_type=MESH,
        )

    def hop(which, src, dst):
        def body(i, carry):
            hop_copy(which, src, dst, i, gy).start()
            return carry

        lax.fori_loop(1, 32, body, 0)

    def hop_recv(which, src, dst):
        def body(i, carry):
            hop_copy(which, src, dst, i, (gy + 32 - i) % 32).wait_recv()
            return carry

        lax.fori_loop(1, 32, body, 0)

    def hop_sent(which, src, dst):
        def body(i, carry):
            hop_copy(which, src, dst, i, gy).wait_send()
            return carry

        lax.fori_loop(1, 32, body, 0)

    hop(0, qa, qrecv)

    loads[6].wait()
    own[...] = cdot(xv[...], wu[3])
    moved[8].wait_recv()
    own[...] += f32(ur[1])

    def gelu_rows(h):
        rows = slice(h * 128, h * 128 + 128)
        moved[4 + h].wait_recv()
        v = own[rows, :] + f32(ux[rows, :])
        v = 0.5 * v * (1.0 + lax.erf(v * 0.7071067811865476))
        act[rows, quarter(gx)] = v.astype(bf)
        here = act.at[rows, quarter(gx)]
        move(9 + h, here, here, far)
        move(13 + h, here, here, core)

    gelu_rows(0)
    gelu_rows(1)

    loads[7].wait()
    hop_recv(0, qa, qrecv)
    qall = qrecv[...].reshape(512, 128)
    k2, j2 = iotas((128, 256))
    spread = cdot(qall, one_hot(k2 - 64 == j2 % 8))
    e3, j3 = iotas((512, 256))
    spread = jnp.where(j3 // 8 == e3 // 16, spread, 0.0).astype(bf)
    b4, e4 = iotas((16, 512))
    fresh = cdot(one_hot(e4 % 16 == b4), spread).astype(bf)
    fr = jnp.concatenate([fresh[:, 0:128], fresh[:, 128:256]], axis=0)
    qp = cdot(perm[...], qall)
    _, lane = iotas((512, 128))
    q128 = jnp.where(lane < 64, qp, 0.0).astype(bf)
    _, pos = iotas((16, 256))
    for b in range(16):
        ln = len_ref[b]
        for a in range(2):
            row = b * 32 + a * 16
            sc = tdot(q128[row : row + 16], kv[b, a]) * 0.125
            ss[row : row + 16, :] = jnp.where(pos < ln, sc, -1e30)
    sn = tdot(q128, fr) * 0.125
    e5, j5 = iotas((512, 32))
    match = j5 == ((e5 // 16) % 2) * 16 + e5 // 32
    sn = jnp.sum(jnp.where(match, sn, 0.0), axis=1, keepdims=True)
    wns = []
    for i in range(4):
        blk = ss[i * 128 : (i + 1) * 128, :]
        new = sn[i * 128 : (i + 1) * 128]
        top = jnp.maximum(jnp.max(blk, axis=1, keepdims=True), new)
        e = jnp.exp(blk - top)
        en = jnp.exp(new - top)
        tot = jnp.sum(e, axis=1, keepdims=True) + en
        wv[i * 128 : (i + 1) * 128, :] = (e / tot).astype(bf)
        wns.append(en / tot)
    wn = jnp.concatenate(wns, axis=0)
    wnm = jnp.where(match, wn, 0.0).astype(bf)
    for b in range(16):
        for a in range(2):
            row = b * 32 + a * 16
            att[row : row + 16, :] = cdot(wv[row : row + 16, :], kv[b, a])
    atted = (att[...] + cdot(wnm, fr)).astype(bf)
    asend[...] = cdot(iperm[...], atted).astype(bf).reshape(32, 16, 128)
    hrecv[gy] = asend[gy]
    hop(1, asend, hrecv)


    gelu_rows(2)
    gelu_rows(3)

    g = (1 - xh) * 2 + c

    def pass_on(h):
        rows = slice(h * 128, h * 128 + 128)
        moved[9 + h].wait_recv()
        there = act.at[rows, quarter(g)]
        move(17 + h, there, there, core)

    pass_on(0)
    pass_on(1)
    hop_recv(1, asend, hrecv)
    hr = hrecv[...].reshape(512, 128)
    heads4[gx] = jnp.concatenate([hr[0:256, 64:128], hr[256:512, 64:128]], axis=1)
    move(21, heads4.at[gx], heads4.at[gx], far)
    move(22, heads4.at[gx], heads4.at[gx], core)
    pass_on(2)
    pass_on(3)
    moved[21].wait_recv()
    move(23, heads4.at[g], heads4.at[g], core)
    moved[22].wait_recv()
    for i in range(13, 21):
        moved[i].wait_recv()
    moved[23].wait_recv()
    for h in range(2):
        act[h * 256 : h * 256 + 256, 1024:1280] = jnp.concatenate(
            [heads4[o][:, h * 64 : h * 64 + 64] for o in range(4)], axis=1
        )

    def at(yy, zz, xx):
        return (gx, (yy * 4 + zz) * 2 + xx)

    ring = (
        (at((y + 1) % 4, z, xl), at((y + 3) % 4, z, xl)),
        (at(y, (z + 1) % 4, xl), at(y, (z + 3) % 4, xl)),
    )
    pair = at(y, z, 1 - xl)
    coord = (y, z)

    copies = {}

    def send(k, i, src, dst, dev):
        cp = pltpu.make_async_remote_copy(
            src_ref=src, dst_ref=dst, send_sem=ssem.at[k, i], recv_sem=rsem.at[k, i], device_id=dev, device_id_type=MESH
        )
        cp.start()
        copies[k, i] = cp

    def step_compute(k):
        s, lo, w = chunks[k]
        cols = pl.ds(lo, w)
        p = coord[s]
        plus, minus = ring[s]
        for ld in late[k]:
            ld.wait()
        acc = cdot(act[...], wd[:, cols])
        acc = acc.astype(jnp.bfloat16)
        for i in range(4):
            for j in range(4):
                row = (i * 4 + j) * 32
                if s == 0:
                    part[i, j, :, cols] = acc[row : row + 32]
                else:
                    part[j, i, :, cols] = acc[row : row + 32]
        far, nxt, prv = (p + 2) % 4, (p + 1) % 4, (p + 3) % 4
        send(k, 0, part.at[far, 0:2, :, cols], r1.at[0, :, :, cols], plus)
        send(k, 1, part.at[far, 2:4, :, cols], r1.at[1, :, :, cols], minus)
        send(k, 2, part.at[nxt, 2:4, :, cols], r1.at[2, :, :, cols], plus)
        send(k, 3, part.at[prv, 0:2, :, cols], r1.at[3, :, :, cols], minus)

    def step_relay1(k):
        s, lo, w = chunks[k]
        cols = pl.ds(lo, w)
        p = coord[s]
        plus, minus = ring[s]
        nxt, prv = (p + 1) % 4, (p + 3) % 4
        copies[k, 0].wait_recv()
        s1[0, :, :, cols] = (f32(r1[0, :, :, cols]) + f32(part[nxt, 0:2, :, cols])).astype(jnp.bfloat16)
        send(k, 4, s1.at[0, :, :, cols], r1.at[4, :, :, cols], plus)
        copies[k, 1].wait_recv()
        s1[1, :, :, cols] = (f32(r1[1, :, :, cols]) + f32(part[prv, 2:4, :, cols])).astype(jnp.bfloat16)
        send(k, 5, s1.at[1, :, :, cols], r1.at[5, :, :, cols], minus)

    def step_second(k):
        s, lo, w = chunks[k]
        cols = pl.ds(lo, w)
        p, q = coord[s], coord[1 - s]
        plus, minus = ring[1 - s]
        copies[k, 2].wait_recv()
        copies[k, 3].wait_recv()
        copies[k, 4].wait_recv()
        a = f32(part[p, 0:2, :, cols]) + f32(r1[4, :, :, cols]) + f32(r1[3, :, :, cols])
        part2[0:2, :, cols] = a.astype(jnp.bfloat16)
        copies[k, 5].wait_recv()
        b = f32(part[p, 2:4, :, cols]) + f32(r1[5, :, :, cols]) + f32(r1[2, :, :, cols])
        part2[2:4, :, cols] = b.astype(jnp.bfloat16)
        far, nxt, prv = (q + 2) % 4, (q + 1) % 4, (q + 3) % 4
        send(k, 6, part2.at[far, 0:16, cols], r2.at[0, :, cols], plus)
        send(k, 7, part2.at[far, 16:32, cols], r2.at[1, :, cols], minus)
        send(k, 8, part2.at[nxt, 16:32, cols], r2.at[2, :, cols], plus)
        send(k, 9, part2.at[prv, 0:16, cols], r2.at[3, :, cols], minus)

    def step_relay2(k):
        s, lo, w = chunks[k]
        cols = pl.ds(lo, w)
        q = coord[1 - s]
        plus, minus = ring[1 - s]
        nxt, prv = (q + 1) % 4, (q + 3) % 4
        copies[k, 6].wait_recv()
        s2[0, :, cols] = (f32(r2[0, :, cols]) + f32(part2[nxt, 0:16, cols])).astype(jnp.bfloat16)
        send(k, 10, s2.at[0, :, cols], r2.at[4, :, cols], plus)
        copies[k, 7].wait_recv()
        s2[1, :, cols] = (f32(r2[1, :, cols]) + f32(part2[prv, 16:32, cols])).astype(jnp.bfloat16)
        send(k, 11, s2.at[1, :, cols], r2.at[5, :, cols], minus)

    def step_pair(k):
        s, lo, w = chunks[k]
        cols = pl.ds(lo, w)
        q = coord[1 - s]
        for i in (8, 9, 10, 11):
            copies[k, i].wait_recv()
        a = f32(part2[q, 0:16, cols]) + f32(r2[4, :, cols]) + f32(r2[3, :, cols])
        b = f32(part2[q, 16:32, cols]) + f32(r2[5, :, cols]) + f32(r2[2, :, cols])
        part3[0, :, cols] = a.astype(jnp.bfloat16)
        part3[1, :, cols] = b.astype(jnp.bfloat16)
        own3[0, :, cols] = a
        own3[1, :, cols] = b
        send(k, 12, part3.at[1 - xl, :, cols], r3.at[:, cols], pair)

    def step_last(k):
        s, lo, w = chunks[k]
        cols = pl.ds(lo, w)
        copies[k, 12].wait_recv()
        out_ref[:, cols] = own3[xl, :, cols] + f32(r3[:, cols])

    steps = (step_compute, step_relay1, step_second, step_relay2, step_pair, step_last)
    n = len(chunks)
    for t in range(n + lag[-1]):
        for fn, d in zip(steps, lag):
            if 0 <= t - d < n:
                fn(t - d)
    for k in range(n):
        for i in range(13):
            copies[k, i].wait_send()
    for i in range(24):
        moved[i].wait_send()
    hop_sent(0, qa, qrecv)
    hop_sent(1, asend, hrecv)


def layer(normed, w_query, w_keyval, w_out, w_up, w_down, kv_cache, lengths, lanes=512, lag=(0, 2, 4, 6, 8, 10)):
    width = normed.shape[1]
    bf, f4 = jnp.bfloat16, jnp.float32
    V = pltpu.VMEM
    wq = jnp.transpose(w_query, (1, 2, 3, 0)).reshape(-1, width)
    wkv = jnp.transpose(w_keyval, (1, 2, 0)).reshape(-1, width)
    kv = kv_cache.reshape(16, 2, 256, 128)
    wo = w_out.reshape(-1, width)
    chunks = column_chunks(width, lanes)
    n = len(chunks)
    hbm = pl.BlockSpec(memory_space=pl.ANY)
    return pl.pallas_call(
        functools.partial(layer_kernel, chunks, lag),
        out_shape=jax.ShapeDtypeStruct((16, width), f4),
        in_specs=[pl.BlockSpec(memory_space=pltpu.SMEM)] + [hbm] * 7,
        out_specs=pl.BlockSpec(memory_space=pltpu.VMEM),
        scratch_shapes=[
            V((512, width), bf),
            V((256, width), bf),
            V((32, width), bf),
            V((4, width, 256), bf),
            V((16, 2, 256, 128), bf),
            V((2, 2, 72, 512), f4),
            V((2, 72, 512), f4),
            V((72, 512), f4),
            V((72, 512), f4),
            V((32, 16, 128), bf),
            V((32, 16, 128), bf),
            V((2, 512, 256), bf),
            V((2, 512, 256), bf),
            V((512, 256), bf),
            V((512, 256), bf),
            V((512, 256), f4),
            V((512, 1280), bf),
            V((512, 512), bf),
            V((512, 512), bf),
            V((512, 256), f4),
            V((512, 256), bf),
            V((512, 128), f4),
            V((32, 16, 128), bf),
            V((32, 16, 128), bf),
            V((4, 256, 128), bf),
            V((1280, width), bf),
            V((4, 4, 32, width), bf),
            V((6, 2, 32, width), bf),
            V((2, 2, 32, width), bf),
            V((4, 32, width), bf),
            V((6, 16, width), bf),
            V((2, 16, width), bf),
            V((2, 16, width), bf),
            V((2, 16, width), f4),
            V((16, width), bf),
            pltpu.SemaphoreType.DMA((8 + 2 * n,)),
            pltpu.SemaphoreType.DMA((24,)),
            pltpu.SemaphoreType.DMA((24,)),
            pltpu.SemaphoreType.DMA((2, 32)),
            pltpu.SemaphoreType.DMA((2, 32)),
            pltpu.SemaphoreType.DMA((n, 13)),
            pltpu.SemaphoreType.DMA((n, 13)),
        ],
        compiler_params=pltpu.CompilerParams(
            collective_id=1, has_side_effects=True, vmem_limit_bytes=60 * 1024 * 1024
        ),
        cost_estimate=pl.CostEstimate(
            flops=2 * 512 * 2592 * width, bytes_accessed=2 * 3200 * width, transcendentals=0
        ),
    )(lengths, normed, wq, wkv, w_up, kv, w_down, wo)


def on_device(normed, residual, w_query, w_keyval, w_out, w_up, w_down, kv_cache, lengths):
    summed = layer(normed, w_query, w_keyval, w_out, w_up, w_down, kv_cache, lengths)
    return (residual.astype(jnp.float32) + summed).astype(jnp.bfloat16)


def solution(mesh):
    placed = (
        P(None, "gx"),
        P("gy", "gx"),
        P("gx", None, "gy", None),
        P("gx", None, "gy"),
        P("gy", None, None, "gx"),
        P("gx", "gy"),
        P("gy", "gx"),
        P("gy", "gx", None, None, None),
        P("gy"),
    )
    return jax.shard_map(
        on_device, mesh=mesh, in_specs=placed, out_specs=P("gy", "gx"), check_vma=False
    )
```

```python
import functools

import jax
import jax.numpy as jnp
from jax import lax
from jax.experimental import pallas as pl
from jax.experimental.pallas import tpu as pltpu
from jax.sharding import PartitionSpec as P

MESH = pl.DeviceIdType.MESH


def cdot(a, b):
    return lax.dot_general(a, b, (((1,), (0,)), ((), ())), preferred_element_type=jnp.float32)


def column_chunks(width, lanes):
    tiles = width // 128
    first = (tiles // 2) // 2 * 2
    cols = []
    for lo, hi in ((0, first * 128), (first * 128, width)):
        parts = []
        while lo < hi:
            w = min(lanes, hi - lo)
            parts.append((lo, w))
            lo += w
        cols.append(parts)
    order = []
    for i in range(max(len(cols[0]), len(cols[1]))):
        for s in (0, 1):
            if i < len(cols[s]):
                order.append((s, cols[s][i][0], cols[s][i][1]))
    return order


def tdot(a, b):
    return lax.dot_general(a, b, (((1,), (1,)), ((), ())), preferred_element_type=jnp.float32)


def iotas(shape):
    return lax.broadcasted_iota(jnp.int32, shape, 0), lax.broadcasted_iota(jnp.int32, shape, 1)


def one_hot(mask):
    return jnp.where(mask, 1.0, 0.0).astype(jnp.bfloat16)


OFFSETS = sorted(
    ((dy, dz, dx) for dy in range(4) for dz in range(4) for dx in range(2) if dy + dz + dx > 0),
    key=lambda d: -(min(d[0], 4 - d[0]) + min(d[1], 4 - d[1]) + d[2]),
)


def layer_kernel(chunks, lag, len_ref, x_hbm, wq_hbm, wkv_hbm, wu_hbm, kv_hbm, wd_hbm, wo_hbm, out_ref,
                 xv, wq, wkv, wu, kv, qpart, qr1, qs, qr2, qa, qrecv, us, ur, xs, ux, own, act, perm, iperm, ss, wv, att, asend,
                 hrecv, heads4, wd, early, part, r1, s1, part2, r2, s2, part3, own3, r3, wsem, fsend, frecv, asem, brecv, ssem, rsem):
    bf = jnp.bfloat16
    gx = lax.axis_index("gx")
    gy = lax.axis_index("gy")
    xh, c = gx // 2, gx % 2
    y, z, xl = gy // 8, (gy // 2) % 4, gy % 2
    core = (xh * 2 + 1 - c, gy)
    far = ((1 - xh) * 2 + c, gy)
    order = ((1 - xh) * 2 + 1 - c, (1 - xh) * 2 + c, xh * 2 + 1 - c, gx)

    def f32(v):
        return v.astype(jnp.float32)

    def quarter(g):
        return pl.ds(pl.multiple_of(g * 256, 256), 256)

    loads = [
        pltpu.make_async_copy(x_hbm, xv, wsem.at[0]),
        pltpu.make_async_copy(wq_hbm, wq, wsem.at[1]),
        pltpu.make_async_copy(wkv_hbm, wkv, wsem.at[2]),
    ]
    for i in range(4):
        loads.append(pltpu.make_async_copy(wu_hbm.at[:, quarter(order[i])], wu.at[i], wsem.at[3 + i]))
    loads.append(pltpu.make_async_copy(kv_hbm, kv, wsem.at[7]))
    for ld in loads[:3]:
        ld.start()
    late = []
    for k, (_, lo, w) in enumerate(chunks):
        cols = pl.ds(lo, w)
        late.append(
            (
                pltpu.make_async_copy(wd_hbm.at[:, cols], wd.at[0:1024, cols], wsem.at[8 + 2 * k]),
                pltpu.make_async_copy(wo_hbm.at[:, cols], wd.at[1024:1280, cols], wsem.at[9 + 2 * k]),
            )
        )

    barrier = pltpu.get_barrier_semaphore()
    pl.semaphore_signal(barrier, inc=1, device_id=core, device_id_type=MESH)
    pl.semaphore_signal(barrier, inc=1, device_id=far, device_id_type=MESH)

    for dy, dz, dx in OFFSETS:
        peer = (((y + dy) % 4) * 4 + (z + dz) % 4) * 2 + (xl + dx) % 2
        pl.semaphore_signal(barrier, inc=1, device_id=(gx, peer), device_id_type=MESH)

    moved = {}

    def move(i, src, dst, dev):
        cp = pltpu.make_async_remote_copy(
            src_ref=src, dst_ref=dst, send_sem=fsend.at[i], recv_sem=frecv.at[i], device_id=dev, device_id_type=MESH
        )
        cp.start()
        moved[i] = cp

    for ld in loads[:3]:
        ld.wait()
    for ld in loads[3:]:
        ld.start()
    qt = tdot(wq[...], xv[...])
    kvt = tdot(wkv[...], xv[...])
    for o in range(4):
        qpart[o // 2, o % 2, 0:64, :] = qt[o * 64 : o * 64 + 64]
        qpart[o // 2, o % 2, 64:72, :] = kvt[o * 8 : o * 8 + 8]
    pl.semaphore_wait(barrier, 33)
    move(0, qpart.at[1 - xh, 1 - c], qr1.at[0], core)
    move(1, qpart.at[xh, 1 - c], qr1.at[1], core)

    loads[3].wait()
    us[0] = cdot(xv[...], wu[0]).astype(bf)
    move(2, us.at[0], ur.at[0], core)

    moved[0].wait_recv()
    qs[...] = qpart[1 - xh, c] + qr1[0]
    move(3, qs, qr2, far)

    loads[4].wait()
    up = cdot(xv[...], wu[1])
    moved[2].wait_recv()
    xs[...] = (up + f32(ur[0])).astype(bf)
    for a, b in late:
        a.start()
        b.start()

    loads[5].wait()
    us[1] = cdot(xv[...], wu[2]).astype(bf)
    move(8, us.at[1], ur.at[1], core)

    r, k = iotas((512, 512))
    perm[...] = one_hot(k == (r % 32) * 16 + r // 32)
    iperm[...] = one_hot(k == (r % 16) * 32 + r // 16)

    moved[1].wait_recv()
    moved[3].wait_recv()
    qsum = qpart[xh, c] + qr1[1] + qr2[...]
    qrows = jnp.concatenate([qsum, jnp.zeros((56, 512), jnp.float32)], axis=0).T
    qa[...] = qrows.astype(bf).reshape(32, 16, 128)
    qrecv[gy] = qa[gy]

    def hop_copy(which, src, dst, i, sending):
        dy, dz, dx = OFFSETS[i]
        peer = (((y + dy) % 4) * 4 + (z + dz) % 4) * 2 + (xl + dx) % 2
        slot = gy if sending else (((y + 4 - dy) % 4) * 4 + (z + 4 - dz) % 4) * 2 + (xl + dx) % 2
        return pltpu.make_async_remote_copy(
            src_ref=src.at[peer],
            dst_ref=dst.at[slot],
            send_sem=asem.at[which, i],
            recv_sem=brecv.at[which, i],
            device_id=(gx, peer),
            device_id_type=MESH,
        )

    def hop(which, src, dst):
        for i in range(31):
            hop_copy(which, src, dst, i, True).start()

    def hop_recv(which, src, dst):
        for i in range(30, -1, -1):
            hop_copy(which, src, dst, i, False).wait_recv()

    def hop_sent(which, src, dst):
        for i in range(31):
            hop_copy(which, src, dst, i, True).wait_send()

    hop(0, qa, qrecv)
    for h in range(4):
        rows = slice(h * 128, h * 128 + 128)
        move(4 + h, xs.at[rows], ux.at[rows], far)


    loads[6].wait()
    own[...] = cdot(xv[...], wu[3])
    moved[8].wait_recv()
    own[...] += f32(ur[1])

    def gelu_rows(h):
        rows = slice(h * 128, h * 128 + 128)
        moved[4 + h].wait_recv()
        v = own[rows, :] + f32(ux[rows, :])
        v = 0.5 * v * (1.0 + lax.erf(v * 0.7071067811865476))
        act[rows, quarter(gx)] = v.astype(bf)
        here = act.at[rows, quarter(gx)]
        move(9 + h, here, here, far)
        move(13 + h, here, here, core)

    gelu_rows(0)
    gelu_rows(1)

    loads[7].wait()
    hop_recv(0, qa, qrecv)
    qall = qrecv[...].reshape(512, 128)
    k2, j2 = iotas((128, 256))
    spread = cdot(qall, one_hot(k2 - 64 == j2 % 8))
    e3, j3 = iotas((512, 256))
    spread = jnp.where(j3 // 8 == e3 // 16, spread, 0.0).astype(bf)
    b4, e4 = iotas((16, 512))
    fresh = cdot(one_hot(e4 % 16 == b4), spread).astype(bf)
    fr = jnp.concatenate([fresh[:, 0:128], fresh[:, 128:256]], axis=0)
    qp = cdot(perm[...], qall)
    _, lane = iotas((512, 128))
    q128 = jnp.where(lane < 64, qp, 0.0).astype(bf)
    _, pos = iotas((16, 256))
    for b in range(16):
        ln = len_ref[b]
        for a in range(2):
            row = b * 32 + a * 16
            sc = tdot(q128[row : row + 16], kv[b, a]) * 0.125
            ss[row : row + 16, :] = jnp.where(pos < ln, sc, -1e30)
    sn = tdot(q128, fr) * 0.125
    e5, j5 = iotas((512, 32))
    match = j5 == ((e5 // 16) % 2) * 16 + e5 // 32
    sn = jnp.sum(jnp.where(match, sn, 0.0), axis=1, keepdims=True)
    wns = []
    for i in range(4):
        blk = ss[i * 128 : (i + 1) * 128, :]
        new = sn[i * 128 : (i + 1) * 128]
        top = jnp.maximum(jnp.max(blk, axis=1, keepdims=True), new)
        e = jnp.exp(blk - top)
        en = jnp.exp(new - top)
        tot = jnp.sum(e, axis=1, keepdims=True) + en
        wv[i * 128 : (i + 1) * 128, :] = (e / tot).astype(bf)
        wns.append(en / tot)
    wn = jnp.concatenate(wns, axis=0)
    wnm = jnp.where(match, wn, 0.0).astype(bf)
    for b in range(16):
        for a in range(2):
            row = b * 32 + a * 16
            att[row : row + 16, :] = cdot(wv[row : row + 16, :], kv[b, a])
    atted = (att[...] + cdot(wnm, fr)).astype(bf)
    asend[...] = cdot(iperm[...], atted).astype(bf).reshape(32, 16, 128)
    hrecv[gy] = asend[gy]
    hop(1, asend, hrecv)


    gelu_rows(2)
    gelu_rows(3)

    g = (1 - xh) * 2 + c

    def pass_on(h):
        rows = slice(h * 128, h * 128 + 128)
        moved[9 + h].wait_recv()
        there = act.at[rows, quarter(g)]
        move(17 + h, there, there, core)

    pass_on(0)
    pass_on(1)
    hop_recv(1, asend, hrecv)
    hr = hrecv[...].reshape(512, 128)
    heads4[gx] = jnp.concatenate([hr[0:256, 64:128], hr[256:512, 64:128]], axis=1)
    move(21, heads4.at[gx], heads4.at[gx], far)
    move(22, heads4.at[gx], heads4.at[gx], core)
    pass_on(2)
    pass_on(3)
    for i in range(13, 21):
        moved[i].wait_recv()

    def ahead(k):
        _, lo, w = chunks[k]
        for ld in late[k]:
            ld.wait()
        early[k, :, 0:w] = cdot(act[:, 0:1024], wd[0:1024, lo : lo + w])

    ahead(0)
    moved[21].wait_recv()
    move(23, heads4.at[g], heads4.at[g], core)
    ahead(1)
    moved[22].wait_recv()
    moved[23].wait_recv()
    for h in range(2):
        act[h * 256 : h * 256 + 256, 1024:1280] = jnp.concatenate(
            [heads4[o][:, h * 64 : h * 64 + 64] for o in range(4)], axis=1
        )

    def at(yy, zz, xx):
        return (gx, (yy * 4 + zz) * 2 + xx)

    ring = (
        (at((y + 1) % 4, z, xl), at((y + 3) % 4, z, xl)),
        (at(y, (z + 1) % 4, xl), at(y, (z + 3) % 4, xl)),
    )
    pair = at(y, z, 1 - xl)
    coord = (y, z)

    copies = {}

    def send(k, i, src, dst, dev):
        cp = pltpu.make_async_remote_copy(
            src_ref=src, dst_ref=dst, send_sem=ssem.at[k, i], recv_sem=rsem.at[k, i], device_id=dev, device_id_type=MESH
        )
        cp.start()
        copies[k, i] = cp

    def step_compute(k):
        s, lo, w = chunks[k]
        cols = pl.ds(lo, w)
        p = coord[s]
        plus, minus = ring[s]
        if k < 2:
            acc = early[k, :, 0:w] + cdot(act[:, 1024:1280], wd[1024:1280, cols])
        else:
            for ld in late[k]:
                ld.wait()
            acc = cdot(act[...], wd[:, cols])
        acc = acc.astype(jnp.bfloat16)
        for i in range(4):
            for j in range(4):
                row = (i * 4 + j) * 32
                if s == 0:
                    part[i, j, :, cols] = acc[row : row + 32]
                else:
                    part[j, i, :, cols] = acc[row : row + 32]
        far, nxt, prv = (p + 2) % 4, (p + 1) % 4, (p + 3) % 4
        send(k, 0, part.at[far, 0:2, :, cols], r1.at[0, :, :, cols], plus)
        send(k, 1, part.at[far, 2:4, :, cols], r1.at[1, :, :, cols], minus)
        send(k, 2, part.at[nxt, 2:4, :, cols], r1.at[2, :, :, cols], plus)
        send(k, 3, part.at[prv, 0:2, :, cols], r1.at[3, :, :, cols], minus)

    def step_relay1(k):
        s, lo, w = chunks[k]
        cols = pl.ds(lo, w)
        p = coord[s]
        plus, minus = ring[s]
        nxt, prv = (p + 1) % 4, (p + 3) % 4
        copies[k, 0].wait_recv()
        s1[0, :, :, cols] = (f32(r1[0, :, :, cols]) + f32(part[nxt, 0:2, :, cols])).astype(jnp.bfloat16)
        send(k, 4, s1.at[0, :, :, cols], r1.at[4, :, :, cols], plus)
        copies[k, 1].wait_recv()
        s1[1, :, :, cols] = (f32(r1[1, :, :, cols]) + f32(part[prv, 2:4, :, cols])).astype(jnp.bfloat16)
        send(k, 5, s1.at[1, :, :, cols], r1.at[5, :, :, cols], minus)

    def step_second(k):
        s, lo, w = chunks[k]
        cols = pl.ds(lo, w)
        p, q = coord[s], coord[1 - s]
        plus, minus = ring[1 - s]
        copies[k, 2].wait_recv()
        copies[k, 3].wait_recv()
        copies[k, 4].wait_recv()
        a = f32(part[p, 0:2, :, cols]) + f32(r1[4, :, :, cols]) + f32(r1[3, :, :, cols])
        part2[0:2, :, cols] = a.astype(jnp.bfloat16)
        copies[k, 5].wait_recv()
        b = f32(part[p, 2:4, :, cols]) + f32(r1[5, :, :, cols]) + f32(r1[2, :, :, cols])
        part2[2:4, :, cols] = b.astype(jnp.bfloat16)
        far, nxt, prv = (q + 2) % 4, (q + 1) % 4, (q + 3) % 4
        send(k, 6, part2.at[far, 0:16, cols], r2.at[0, :, cols], plus)
        send(k, 7, part2.at[far, 16:32, cols], r2.at[1, :, cols], minus)
        send(k, 8, part2.at[nxt, 16:32, cols], r2.at[2, :, cols], plus)
        send(k, 9, part2.at[prv, 0:16, cols], r2.at[3, :, cols], minus)

    def step_relay2(k):
        s, lo, w = chunks[k]
        cols = pl.ds(lo, w)
        q = coord[1 - s]
        plus, minus = ring[1 - s]
        nxt, prv = (q + 1) % 4, (q + 3) % 4
        copies[k, 6].wait_recv()
        s2[0, :, cols] = (f32(r2[0, :, cols]) + f32(part2[nxt, 0:16, cols])).astype(jnp.bfloat16)
        send(k, 10, s2.at[0, :, cols], r2.at[4, :, cols], plus)
        copies[k, 7].wait_recv()
        s2[1, :, cols] = (f32(r2[1, :, cols]) + f32(part2[prv, 16:32, cols])).astype(jnp.bfloat16)
        send(k, 11, s2.at[1, :, cols], r2.at[5, :, cols], minus)

    def step_pair(k):
        s, lo, w = chunks[k]
        cols = pl.ds(lo, w)
        q = coord[1 - s]
        for i in (8, 9, 10, 11):
            copies[k, i].wait_recv()
        a = f32(part2[q, 0:16, cols]) + f32(r2[4, :, cols]) + f32(r2[3, :, cols])
        b = f32(part2[q, 16:32, cols]) + f32(r2[5, :, cols]) + f32(r2[2, :, cols])
        part3[0, :, cols] = a.astype(jnp.bfloat16)
        part3[1, :, cols] = b.astype(jnp.bfloat16)
        own3[0, :, cols] = a
        own3[1, :, cols] = b
        send(k, 12, part3.at[1 - xl, :, cols], r3.at[:, cols], pair)

    def step_last(k):
        s, lo, w = chunks[k]
        cols = pl.ds(lo, w)
        copies[k, 12].wait_recv()
        out_ref[:, cols] = own3[xl, :, cols] + f32(r3[:, cols])

    steps = (step_compute, step_relay1, step_second, step_relay2, step_pair, step_last)
    n = len(chunks)
    for t in range(n + lag[-1]):
        for fn, d in zip(steps, lag):
            if 0 <= t - d < n:
                fn(t - d)
    for k in range(n):
        for i in range(13):
            copies[k, i].wait_send()
    for i in range(24):
        moved[i].wait_send()
    hop_sent(0, qa, qrecv)
    hop_sent(1, asend, hrecv)


def layer(normed, w_query, w_keyval, w_out, w_up, w_down, kv_cache, lengths, lanes=1024, lag=(0, 2, 4, 6, 8, 10)):
    width = normed.shape[1]
    bf, f4 = jnp.bfloat16, jnp.float32
    V = pltpu.VMEM
    wq = jnp.transpose(w_query, (1, 2, 3, 0)).reshape(-1, width)
    wkv = jnp.transpose(w_keyval, (1, 2, 0)).reshape(-1, width)
    kv = kv_cache.reshape(16, 2, 256, 128)
    wo = w_out.reshape(-1, width)
    chunks = column_chunks(width, lanes)
    n = len(chunks)
    hbm = pl.BlockSpec(memory_space=pl.ANY)
    return pl.pallas_call(
        functools.partial(layer_kernel, chunks, lag),
        out_shape=jax.ShapeDtypeStruct((16, width), f4),
        in_specs=[pl.BlockSpec(memory_space=pltpu.SMEM)] + [hbm] * 7,
        out_specs=pl.BlockSpec(memory_space=pltpu.VMEM),
        scratch_shapes=[
            V((512, width), bf),
            V((256, width), bf),
            V((32, width), bf),
            V((4, width, 256), bf),
            V((16, 2, 256, 128), bf),
            V((2, 2, 72, 512), f4),
            V((2, 72, 512), f4),
            V((72, 512), f4),
            V((72, 512), f4),
            V((32, 16, 128), bf),
            V((32, 16, 128), bf),
            V((2, 512, 256), bf),
            V((2, 512, 256), bf),
            V((512, 256), bf),
            V((512, 256), bf),
            V((512, 256), f4),
            V((512, 1280), bf),
            V((512, 512), bf),
            V((512, 512), bf),
            V((512, 256), f4),
            V((512, 256), bf),
            V((512, 128), f4),
            V((32, 16, 128), bf),
            V((32, 16, 128), bf),
            V((4, 256, 128), bf),
            V((1280, width), bf),
            V((2, 512, lanes), f4),
            V((4, 4, 32, width), bf),
            V((6, 2, 32, width), bf),
            V((2, 2, 32, width), bf),
            V((4, 32, width), bf),
            V((6, 16, width), bf),
            V((2, 16, width), bf),
            V((2, 16, width), bf),
            V((2, 16, width), f4),
            V((16, width), bf),
            pltpu.SemaphoreType.DMA((8 + 2 * n,)),
            pltpu.SemaphoreType.DMA((24,)),
            pltpu.SemaphoreType.DMA((24,)),
            pltpu.SemaphoreType.DMA((2, 32)),
            pltpu.SemaphoreType.DMA((2, 32)),
            pltpu.SemaphoreType.DMA((n, 13)),
            pltpu.SemaphoreType.DMA((n, 13)),
        ],
        compiler_params=pltpu.CompilerParams(
            collective_id=1, has_side_effects=True, vmem_limit_bytes=60 * 1024 * 1024
        ),
        cost_estimate=pl.CostEstimate(
            flops=2 * 512 * 2592 * width, bytes_accessed=2 * 3200 * width, transcendentals=0
        ),
    )(lengths, normed, wq, wkv, w_up, kv, w_down, wo)


def on_device(normed, residual, w_query, w_keyval, w_out, w_up, w_down, kv_cache, lengths):
    summed = layer(normed, w_query, w_keyval, w_out, w_up, w_down, kv_cache, lengths)
    return (residual.astype(jnp.float32) + summed).astype(jnp.bfloat16)


def solution(mesh):
    placed = (
        P(None, "gx"),
        P("gy", "gx"),
        P("gx", None, "gy", None),
        P("gx", None, "gy"),
        P("gy", None, None, "gx"),
        P("gx", "gy"),
        P("gy", "gx"),
        P("gy", "gx", None, None, None),
        P("gy"),
    )
    return jax.shard_map(
        on_device, mesh=mesh, in_specs=placed, out_specs=P("gy", "gx"), check_vma=False
    )
```

```python
import functools

import jax
import jax.numpy as jnp
from jax import lax
from jax.experimental import pallas as pl
from jax.experimental.pallas import tpu as pltpu
from jax.sharding import PartitionSpec as P

MESH = pl.DeviceIdType.MESH


def cdot(a, b):
    return lax.dot_general(a, b, (((1,), (0,)), ((), ())), preferred_element_type=jnp.float32)


def column_chunks(width, lanes):
    tiles = width // 128
    first = (tiles // 2) // 2 * 2
    cols = []
    for lo, hi in ((0, first * 128), (first * 128, width)):
        parts = []
        while lo < hi:
            w = min(lanes, hi - lo)
            parts.append((lo, w))
            lo += w
        cols.append(parts)
    order = []
    for i in range(max(len(cols[0]), len(cols[1]))):
        for s in (0, 1):
            if i < len(cols[s]):
                order.append((s, cols[s][i][0], cols[s][i][1]))
    return order


def tdot(a, b):
    return lax.dot_general(a, b, (((1,), (1,)), ((), ())), preferred_element_type=jnp.float32)


def iotas(shape):
    return lax.broadcasted_iota(jnp.int32, shape, 0), lax.broadcasted_iota(jnp.int32, shape, 1)


def one_hot(mask):
    return jnp.where(mask, 1.0, 0.0).astype(jnp.bfloat16)


OFFSETS = sorted(
    ((dy, dz, dx) for dy in range(4) for dz in range(4) for dx in range(2) if dy + dz + dx > 0),
    key=lambda d: -(min(d[0], 4 - d[0]) + min(d[1], 4 - d[1]) + d[2]),
)


PLANE = ((2, 1), (2, 0), (1, 1), (3, 1), (1, 0), (3, 0), (0, 1))


def layer_kernel(chunks, lag, len_ref, x_hbm, wq_hbm, wkv_hbm, wu_hbm, kv_hbm, wd_hbm, wo_hbm, out_ref,
                 xv, wq, wkv, wu, kv, qpart, qr1, qs, qr2, qa, qrecv, us, ur, xs, ux, own, act, perm, iperm, ss, wv, att, asend,
                 hrecv, heads4, wd, early, part, r1, s1, part2, r2, wsem, fsend, frecv, asem, brecv, ssem, rsem):
    bf = jnp.bfloat16
    gx = lax.axis_index("gx")
    gy = lax.axis_index("gy")
    xh, c = gx // 2, gx % 2
    y, z, xl = gy // 8, (gy // 2) % 4, gy % 2
    core = (xh * 2 + 1 - c, gy)
    far = ((1 - xh) * 2 + c, gy)
    order = ((1 - xh) * 2 + 1 - c, (1 - xh) * 2 + c, xh * 2 + 1 - c, gx)

    def f32(v):
        return v.astype(jnp.float32)

    def quarter(g):
        return pl.ds(pl.multiple_of(g * 256, 256), 256)

    loads = [
        pltpu.make_async_copy(x_hbm, xv, wsem.at[0]),
        pltpu.make_async_copy(wq_hbm, wq, wsem.at[1]),
        pltpu.make_async_copy(wkv_hbm, wkv, wsem.at[2]),
    ]
    for i in range(4):
        loads.append(pltpu.make_async_copy(wu_hbm.at[:, quarter(order[i])], wu.at[i], wsem.at[3 + i]))
    loads.append(pltpu.make_async_copy(kv_hbm, kv, wsem.at[7]))
    for ld in loads[:3]:
        ld.start()
    late = []
    for k, (_, lo, w) in enumerate(chunks):
        cols = pl.ds(lo, w)
        late.append(
            (
                pltpu.make_async_copy(wd_hbm.at[:, cols], wd.at[0:1024, cols], wsem.at[8 + 2 * k]),
                pltpu.make_async_copy(wo_hbm.at[:, cols], wd.at[1024:1280, cols], wsem.at[9 + 2 * k]),
            )
        )

    barrier = pltpu.get_barrier_semaphore()
    pl.semaphore_signal(barrier, inc=1, device_id=core, device_id_type=MESH)
    pl.semaphore_signal(barrier, inc=1, device_id=far, device_id_type=MESH)

    for dy, dz, dx in OFFSETS:
        peer = (((y + dy) % 4) * 4 + (z + dz) % 4) * 2 + (xl + dx) % 2
        pl.semaphore_signal(barrier, inc=1, device_id=(gx, peer), device_id_type=MESH)

    moved = {}

    def move(i, src, dst, dev):
        cp = pltpu.make_async_remote_copy(
            src_ref=src, dst_ref=dst, send_sem=fsend.at[i], recv_sem=frecv.at[i], device_id=dev, device_id_type=MESH
        )
        cp.start()
        moved[i] = cp

    for ld in loads[:3]:
        ld.wait()
    for ld in loads[3:]:
        ld.start()
    qt = tdot(wq[...], xv[...])
    kvt = tdot(wkv[...], xv[...])
    for o in range(4):
        qpart[o // 2, o % 2, 0:64, :] = qt[o * 64 : o * 64 + 64]
        qpart[o // 2, o % 2, 64:72, :] = kvt[o * 8 : o * 8 + 8]
    pl.semaphore_wait(barrier, 33)
    move(0, qpart.at[1 - xh, 1 - c], qr1.at[0], core)
    move(1, qpart.at[xh, 1 - c], qr1.at[1], core)

    loads[3].wait()
    us[0] = cdot(xv[...], wu[0]).astype(bf)
    move(2, us.at[0], ur.at[0], core)

    moved[0].wait_recv()
    qs[...] = qpart[1 - xh, c] + qr1[0]
    move(3, qs, qr2, far)

    loads[4].wait()
    up = cdot(xv[...], wu[1])
    moved[2].wait_recv()
    xs[...] = (up + f32(ur[0])).astype(bf)
    for a, b in late:
        a.start()
        b.start()

    loads[5].wait()
    us[1] = cdot(xv[...], wu[2]).astype(bf)
    move(8, us.at[1], ur.at[1], core)

    r, k = iotas((512, 512))
    perm[...] = one_hot(k == (r % 32) * 16 + r // 32)
    iperm[...] = one_hot(k == (r % 16) * 32 + r // 16)

    moved[1].wait_recv()
    moved[3].wait_recv()
    qsum = qpart[xh, c] + qr1[1] + qr2[...]
    qrows = jnp.concatenate([qsum, jnp.zeros((56, 512), jnp.float32)], axis=0).T
    qa[...] = qrows.astype(bf).reshape(32, 16, 128)
    qrecv[gy] = qa[gy]

    def hop_copy(which, src, dst, i, sending):
        dy, dz, dx = OFFSETS[i]
        peer = (((y + dy) % 4) * 4 + (z + dz) % 4) * 2 + (xl + dx) % 2
        slot = gy if sending else (((y + 4 - dy) % 4) * 4 + (z + 4 - dz) % 4) * 2 + (xl + dx) % 2
        return pltpu.make_async_remote_copy(
            src_ref=src.at[peer],
            dst_ref=dst.at[slot],
            send_sem=asem.at[which, i],
            recv_sem=brecv.at[which, i],
            device_id=(gx, peer),
            device_id_type=MESH,
        )

    def hop(which, src, dst):
        for i in range(31):
            hop_copy(which, src, dst, i, True).start()

    def hop_recv(which, src, dst):
        for i in range(30, -1, -1):
            hop_copy(which, src, dst, i, False).wait_recv()

    def hop_sent(which, src, dst):
        for i in range(31):
            hop_copy(which, src, dst, i, True).wait_send()

    hop(0, qa, qrecv)
    for h in range(4):
        rows = slice(h * 128, h * 128 + 128)
        move(4 + h, xs.at[rows], ux.at[rows], far)


    loads[6].wait()
    own[...] = cdot(xv[...], wu[3])
    moved[8].wait_recv()
    own[...] += f32(ur[1])

    def gelu_rows(h):
        rows = slice(h * 128, h * 128 + 128)
        moved[4 + h].wait_recv()
        v = own[rows, :] + f32(ux[rows, :])
        v = 0.5 * v * (1.0 + lax.erf(v * 0.7071067811865476))
        act[rows, quarter(gx)] = v.astype(bf)
        here = act.at[rows, quarter(gx)]
        move(9 + h, here, here, far)
        move(13 + h, here, here, core)

    gelu_rows(0)
    gelu_rows(1)

    loads[7].wait()
    hop_recv(0, qa, qrecv)
    qall = qrecv[...].reshape(512, 128)
    k2, j2 = iotas((128, 256))
    spread = cdot(qall, one_hot(k2 - 64 == j2 % 8))
    e3, j3 = iotas((512, 256))
    spread = jnp.where(j3 // 8 == e3 // 16, spread, 0.0).astype(bf)
    b4, e4 = iotas((16, 512))
    fresh = cdot(one_hot(e4 % 16 == b4), spread).astype(bf)
    fr = jnp.concatenate([fresh[:, 0:128], fresh[:, 128:256]], axis=0)
    qp = cdot(perm[...], qall)
    _, lane = iotas((512, 128))
    q128 = jnp.where(lane < 64, qp, 0.0).astype(bf)
    _, pos = iotas((16, 256))
    for b in range(16):
        ln = len_ref[b]
        for a in range(2):
            row = b * 32 + a * 16
            sc = tdot(q128[row : row + 16], kv[b, a]) * 0.125
            ss[row : row + 16, :] = jnp.where(pos < ln, sc, -1e30)
    sn = tdot(q128, fr) * 0.125
    e5, j5 = iotas((512, 32))
    match = j5 == ((e5 // 16) % 2) * 16 + e5 // 32
    sn = jnp.sum(jnp.where(match, sn, 0.0), axis=1, keepdims=True)
    wns = []
    for i in range(4):
        blk = ss[i * 128 : (i + 1) * 128, :]
        new = sn[i * 128 : (i + 1) * 128]
        top = jnp.maximum(jnp.max(blk, axis=1, keepdims=True), new)
        e = jnp.exp(blk - top)
        en = jnp.exp(new - top)
        tot = jnp.sum(e, axis=1, keepdims=True) + en
        wv[i * 128 : (i + 1) * 128, :] = (e / tot).astype(bf)
        wns.append(en / tot)
    wn = jnp.concatenate(wns, axis=0)
    wnm = jnp.where(match, wn, 0.0).astype(bf)
    for b in range(16):
        for a in range(2):
            row = b * 32 + a * 16
            att[row : row + 16, :] = cdot(wv[row : row + 16, :], kv[b, a])
    atted = (att[...] + cdot(wnm, fr)).astype(bf)
    asend[...] = cdot(iperm[...], atted).astype(bf).reshape(32, 16, 128)
    hrecv[gy] = asend[gy]
    hop(1, asend, hrecv)


    gelu_rows(2)
    gelu_rows(3)

    g = (1 - xh) * 2 + c

    def pass_on(h):
        rows = slice(h * 128, h * 128 + 128)
        moved[9 + h].wait_recv()
        there = act.at[rows, quarter(g)]
        move(17 + h, there, there, core)

    pass_on(0)
    pass_on(1)
    hop_recv(1, asend, hrecv)
    hr = hrecv[...].reshape(512, 128)
    heads4[gx] = jnp.concatenate([hr[0:256, 64:128], hr[256:512, 64:128]], axis=1)
    move(21, heads4.at[gx], heads4.at[gx], far)
    move(22, heads4.at[gx], heads4.at[gx], core)
    pass_on(2)
    pass_on(3)
    for i in range(13, 21):
        moved[i].wait_recv()

    def ahead(k):
        _, lo, w = chunks[k]
        for ld in late[k]:
            ld.wait()
        early[k, :, 0:w] = cdot(act[:, 0:1024], wd[0:1024, lo : lo + w])

    ahead(0)
    moved[21].wait_recv()
    move(23, heads4.at[g], heads4.at[g], core)
    ahead(1)
    moved[22].wait_recv()
    moved[23].wait_recv()
    for h in range(2):
        act[h * 256 : h * 256 + 256, 1024:1280] = jnp.concatenate(
            [heads4[o][:, h * 64 : h * 64 + 64] for o in range(4)], axis=1
        )

    def at(yy, zz, xx):
        return (gx, (yy * 4 + zz) * 2 + xx)

    ring = (
        (at((y + 1) % 4, z, xl), at((y + 3) % 4, z, xl)),
        (at(y, (z + 1) % 4, xl), at(y, (z + 3) % 4, xl)),
    )
    coord = (y, z)

    copies = {}

    def send(k, i, src, dst, dev):
        cp = pltpu.make_async_remote_copy(
            src_ref=src, dst_ref=dst, send_sem=ssem.at[k, i], recv_sem=rsem.at[k, i], device_id=dev, device_id_type=MESH
        )
        cp.start()
        copies[k, i] = cp

    def step_compute(k):
        s, lo, w = chunks[k]
        cols = pl.ds(lo, w)
        p = coord[s]
        plus, minus = ring[s]
        if k < 2:
            acc = early[k, :, 0:w] + cdot(act[:, 1024:1280], wd[1024:1280, cols])
        else:
            for ld in late[k]:
                ld.wait()
            acc = cdot(act[...], wd[:, cols])
        acc = acc.astype(jnp.bfloat16)
        for i in range(4):
            for j in range(4):
                row = (i * 4 + j) * 32
                if s == 0:
                    part[i, j, :, cols] = acc[row : row + 32]
                else:
                    part[j, i, :, cols] = acc[row : row + 32]
        far, nxt, prv = (p + 2) % 4, (p + 1) % 4, (p + 3) % 4
        send(k, 0, part.at[far, 0:2, :, cols], r1.at[0, :, :, cols], plus)
        send(k, 1, part.at[far, 2:4, :, cols], r1.at[1, :, :, cols], minus)
        send(k, 2, part.at[nxt, 2:4, :, cols], r1.at[2, :, :, cols], plus)
        send(k, 3, part.at[prv, 0:2, :, cols], r1.at[3, :, :, cols], minus)

    def step_relay1(k):
        s, lo, w = chunks[k]
        cols = pl.ds(lo, w)
        p = coord[s]
        plus, minus = ring[s]
        nxt, prv = (p + 1) % 4, (p + 3) % 4
        copies[k, 0].wait_recv()
        s1[0, :, :, cols] = (f32(r1[0, :, :, cols]) + f32(part[nxt, 0:2, :, cols])).astype(jnp.bfloat16)
        send(k, 4, s1.at[0, :, :, cols], r1.at[4, :, :, cols], plus)
        copies[k, 1].wait_recv()
        s1[1, :, :, cols] = (f32(r1[1, :, :, cols]) + f32(part[prv, 2:4, :, cols])).astype(jnp.bfloat16)
        send(k, 5, s1.at[1, :, :, cols], r1.at[5, :, :, cols], minus)

    def step_second(k):
        s, lo, w = chunks[k]
        cols = pl.ds(lo, w)
        p, q = coord[s], coord[1 - s]
        copies[k, 2].wait_recv()
        copies[k, 3].wait_recv()
        copies[k, 4].wait_recv()
        a = f32(part[p, 0:2, :, cols]) + f32(r1[4, :, :, cols]) + f32(r1[3, :, :, cols])
        part2[0:2, :, :, cols] = a.astype(bf).reshape(2, 2, 16, w)
        copies[k, 5].wait_recv()
        b = f32(part[p, 2:4, :, cols]) + f32(r1[5, :, :, cols]) + f32(r1[2, :, :, cols])
        part2[2:4, :, :, cols] = b.astype(bf).reshape(2, 2, 16, w)
        for i, (dq, dx) in enumerate(PLANE):
            there, other = (q + dq) % 4, (xl + dx) % 2
            dev = at(y, there, other) if s == 0 else at(there, z, other)
            send(k, 6 + i, part2.at[there, other, :, cols], r2.at[i, :, cols], dev)

    def step_last(k):
        s, lo, w = chunks[k]
        cols = pl.ds(lo, w)
        q = coord[1 - s]
        total = f32(part2[q, xl, :, cols])
        for i in range(6, -1, -1):
            copies[k, 6 + i].wait_recv()
            total += f32(r2[i, :, cols])
        out_ref[:, cols] = total

    steps = (step_compute, step_relay1, step_second, step_last)
    n = len(chunks)
    ends = n + lag[-1]
    for t in range(ends):
        if t == n:
            for i in range(24):
                moved[i].wait_send()
            hop_sent(0, qa, qrecv)
            hop_sent(1, asend, hrecv)
        if t == ends - 1:
            for k in range(n):
                for i in range(13):
                    copies[k, i].wait_send()
        for fn, d in zip(steps, lag):
            if 0 <= t - d < n:
                fn(t - d)


def layer(normed, w_query, w_keyval, w_out, w_up, w_down, kv_cache, lengths, lanes=1024, lag=(0, 2, 4, 6)):
    width = normed.shape[1]
    bf, f4 = jnp.bfloat16, jnp.float32
    V = pltpu.VMEM
    wq = jnp.transpose(w_query, (1, 2, 3, 0)).reshape(-1, width)
    wkv = jnp.transpose(w_keyval, (1, 2, 0)).reshape(-1, width)
    kv = kv_cache.reshape(16, 2, 256, 128)
    wo = w_out.reshape(-1, width)
    chunks = column_chunks(width, lanes)
    n = len(chunks)
    hbm = pl.BlockSpec(memory_space=pl.ANY)
    return pl.pallas_call(
        functools.partial(layer_kernel, chunks, lag),
        out_shape=jax.ShapeDtypeStruct((16, width), f4),
        in_specs=[pl.BlockSpec(memory_space=pltpu.SMEM)] + [hbm] * 7,
        out_specs=pl.BlockSpec(memory_space=pltpu.VMEM),
        scratch_shapes=[
            V((512, width), bf),
            V((256, width), bf),
            V((32, width), bf),
            V((4, width, 256), bf),
            V((16, 2, 256, 128), bf),
            V((2, 2, 72, 512), f4),
            V((2, 72, 512), f4),
            V((72, 512), f4),
            V((72, 512), f4),
            V((32, 16, 128), bf),
            V((32, 16, 128), bf),
            V((2, 512, 256), bf),
            V((2, 512, 256), bf),
            V((512, 256), bf),
            V((512, 256), bf),
            V((512, 256), f4),
            V((512, 1280), bf),
            V((512, 512), bf),
            V((512, 512), bf),
            V((512, 256), f4),
            V((512, 256), bf),
            V((512, 128), f4),
            V((32, 16, 128), bf),
            V((32, 16, 128), bf),
            V((4, 256, 128), bf),
            V((1280, width), bf),
            V((2, 512, lanes), f4),
            V((4, 4, 32, width), bf),
            V((6, 2, 32, width), bf),
            V((2, 2, 32, width), bf),
            V((4, 2, 16, width), bf),
            V((7, 16, width), bf),
            pltpu.SemaphoreType.DMA((8 + 2 * n,)),
            pltpu.SemaphoreType.DMA((24,)),
            pltpu.SemaphoreType.DMA((24,)),
            pltpu.SemaphoreType.DMA((2, 32)),
            pltpu.SemaphoreType.DMA((2, 32)),
            pltpu.SemaphoreType.DMA((n, 13)),
            pltpu.SemaphoreType.DMA((n, 13)),
        ],
        compiler_params=pltpu.CompilerParams(
            collective_id=1, has_side_effects=True, vmem_limit_bytes=60 * 1024 * 1024
        ),
        cost_estimate=pl.CostEstimate(
            flops=2 * 512 * 2592 * width, bytes_accessed=2 * 3200 * width, transcendentals=0
        ),
    )(lengths, normed, wq, wkv, w_up, kv, w_down, wo)


def on_device(normed, residual, w_query, w_keyval, w_out, w_up, w_down, kv_cache, lengths):
    summed = layer(normed, w_query, w_keyval, w_out, w_up, w_down, kv_cache, lengths)
    return (residual.astype(jnp.float32) + summed).astype(jnp.bfloat16)


def solution(mesh):
    placed = (
        P(None, "gx"),
        P("gy", "gx"),
        P("gx", None, "gy", None),
        P("gx", None, "gy"),
        P("gy", None, None, "gx"),
        P("gx", "gy"),
        P("gy", "gx"),
        P("gy", "gx", None, None, None),
        P("gy"),
    )
    return jax.shard_map(
        on_device, mesh=mesh, in_specs=placed, out_specs=P("gy", "gx"), check_vma=False
    )
```
